32 devices in a mesh: dp: 8 (over y, x, core), tensor: 4 (over z).
Axes of the slice: x: 2, y: 2, z: 4, core: 2. Of those that a mesh axis runs over, the one named last changes fastest.
Arguments:
- inputs: bfloat16 [1024, 16, 768], P('tensor', 'dp'), may hold values from -6 to 6
- qkv_weight: bfloat16 [768, 3, 768], P(None, None, 'tensor'), may hold values from -0.21875 to 0.21875
- qv_bias: bfloat16 [2, 768], P(None, 'tensor'), may hold values from -1.796875 to 1.796875
- out_weight: bfloat16 [768, 768], P('tensor'), may hold values from -0.875 to 0.875
- out_bias: bfloat16 [768], replicated, may hold values from -1.796875 to 1.796875
- first_gain: bfloat16 [768], replicated, may hold values from 0.5 to 1.5
- first_shift: bfloat16 [768], replicated, may hold values from -1.796875 to 1.796875
- first_layer_weight: bfloat16 [768, 3072], P(None, 'tensor'), may hold values from -0.21875 to 0.21875
- first_layer_bias: bfloat16 [3072], P('tensor'), may hold values from -1.796875 to 1.796875
- second_layer_weight: bfloat16 [3072, 768], P('tensor'), may hold values from -0.15625 to 0.15625
- second_layer_bias: bfloat16 [768], replicated, may hold values from -1.796875 to 1.796875
- second_gain: bfloat16 [768], replicated, may hold values from 0.5 to 1.5
- second_shift: bfloat16 [768], replicated, may hold values from -1.796875 to 1.796875
- cluster_order: int32 [16, 12, 1024], P('dp', 'tensor'), may hold values from 0 to 1023, each once within a row
- masked_rows: int32 [16, 154], P('dp'), may hold values from 0 to 1023, as said below
- masked_grad: bfloat16 [16, 154, 768], P('dp'), may hold values from -6 to 6
Outputs:
- outputs: bfloat16 [1024, 16, 768], P('tensor', 'dp')
- grad_inputs: float32 [1024, 16, 768], P('tensor', 'dp')
- grad_qkvweight: float32 [768, 3, 768], P(None, None, 'tensor')
- grad_qvbias: float32 [2, 768], P(None, 'tensor')
- grad_outweight: float32 [768, 768], P('tensor')
- grad_outbias: float32 [768], replicated
- grad_firstgain: float32 [768], replicated
- grad_firstshift: float32 [768], replicated
- grad_upweight: float32 [768, 3072], P(None, 'tensor')
- grad_upbias: float32 [3072], P('tensor')
- grad_downweight: float32 [3072, 768], P('tensor')
- grad_downbias: float32 [768], replicated
- grad_secondgain: float32 [768], replicated
- grad_secondshift: float32 [768], replicated
The draws below stay inside these ranges and needn't reach their ends.
Inputs may be any that keep to these rules, and one draw needn't show every extreme that they name: cluster_order[s, h] lists every position of sequence s exactly once. `masked_rows`: the positions of one sequence are distinct.
All inputs are finite; a program needn't handle non-finite values.
Results may differ from the reference program's by a relative error of at most 0.017.
Values may be sent and summed in bfloat16 or wider, within the bound.
A program may use at most 128 MiB of HBM per device.

```python
import math
import jax
import jax.numpy as jnp
from jax import lax

D = 768
H = 12
HD = 64
FF = 3072
L = 1024
C = 128
MASKED = 154
SEQS = 16


def draw_masked_rows(key, part):
    seq_keys = jax.random.split(key, SEQS)
    picked_tokens = jax.vmap(lambda seq_key: jax.random.permutation(seq_key, L)[:MASKED])(seq_keys)
    return picked_tokens.astype(jnp.int32)


def level_of(key, extent, shards, smallest, largest):
    def one(position, parts):
        draws = jax.random.uniform(jax.random.fold_in(jax.random.fold_in(key, 6), position), (parts,), jnp.float32, smallest / len(shards), largest / len(shards))
        return jnp.repeat(jnp.exp(draws), extent[position] // parts).reshape((-1,) + (1,) * (len(extent) - position - 1))

    factor_of = one(*shards[0])
    for cut in shards[1:]:
        factor_of = factor_of * one(*cut)
    return factor_of


def gaussian(stream_key, shape, scale, limit, cuts=(), kind=jnp.bfloat16):
    loudness = level_of(stream_key, shape, cuts, -0.22, 0.18) if cuts else 1.0
    entries = jax.random.normal(stream_key, shape, jnp.float32) * scale * loudness
    return jnp.minimum(jnp.maximum(entries, -limit), limit).astype(kind)


def setup_inputs(seed: int = 0) -> dict:
    key_of = jax.random.split(jax.random.key(seed), 17)
    inputs = gaussian(key_of[0], (L, SEQS, D), 1.0, 6.0, ((0, 4), (1, 8)))
    qkv_weight = gaussian(key_of[1], (D, 3, D), D ** -0.5, 0.21875, ((2, 4),))
    qv_bias = gaussian(key_of[2], (2, D), 0.3, 1.796875, ((1, 4),))
    out_weight = gaussian(key_of[3], (D, D), (D // 16) ** -0.5, 0.875, ((0, 4),))
    out_bias = gaussian(key_of[4], (D,), 0.3, 1.796875)
    first_gain = jnp.clip(1.0 + 0.1 * jax.random.normal(key_of[5], (D,), jnp.float32), 0.5, 1.5).astype(jnp.bfloat16)
    first_shift = gaussian(key_of[6], (D,), 0.3, 1.796875)
    first_layer_weight = gaussian(key_of[7], (D, FF), D ** -0.5, 0.21875, ((1, 4),))
    first_layer_bias = gaussian(key_of[8], (FF,), 0.3, 1.796875, ((0, 4),))
    second_layer_weight = gaussian(key_of[9], (FF, D), (FF // 2) ** -0.5, 0.15625, ((0, 4),))
    second_layer_bias = gaussian(key_of[10], (D,), 0.3, 1.796875)
    second_gain = jnp.clip(1.0 + 0.1 * jax.random.normal(key_of[11], (D,), jnp.float32), 0.5, 1.5).astype(jnp.bfloat16)
    second_shift = gaussian(key_of[12], (D,), 0.3, 1.796875)
    cluster_order = jax.vmap(lambda own: jax.random.permutation(own, L))(jax.random.split(key_of[13], SEQS * H)).reshape((SEQS, H, L)).astype(jnp.int32)
    masked_rows = draw_masked_rows(jax.random.fold_in(key_of[16], 71), 0)
    masked_grad = gaussian(key_of[15], (SEQS, MASKED, D), 1.0, 6.0, ((0, 8),))
    return {"inputs": inputs, "qkv_weight": qkv_weight, "qv_bias": qv_bias, "out_weight": out_weight, "out_bias": out_bias, "first_gain": first_gain, "first_shift": first_shift, "first_layer_weight": first_layer_weight, "first_layer_bias": first_layer_bias, "second_layer_weight": second_layer_weight, "second_layer_bias": second_layer_bias, "second_gain": second_gain, "second_shift": second_shift, "cluster_order": cluster_order, "masked_rows": masked_rows, "masked_grad": masked_grad}


HIGHEST_ACCURACY = lax.Precision.HIGHEST
NORM_EPS = 1e-05

@jax.custom_vjp
def reduced_copy(v):
    return lax.optimization_barrier(v.astype(jnp.bfloat16)).astype(jnp.float32)

@jax.custom_vjp
def reduced_restore(v):
    return v

def low_keep(v):
    return (reduced_copy(v), None)

def low_pass(kept, grad):
    return (grad,)

def back_keep(v):
    return (v, None)

def back_low(kept, grad):
    return (reduced_copy(grad),)
reduced_copy.defvjp(low_keep, low_pass)
reduced_restore.defvjp(back_keep, back_low)

def layer_norm(values, gain, shift):
    center = values - lax.optimization_barrier(jnp.mean(values, axis=-1, keepdims=True))
    spread = lax.optimization_barrier(jnp.mean(center * center, axis=-1, keepdims=True))
    return center * lax.rsqrt(spread + NORM_EPS) * gain + shift

def head_attention(query, keyed, valued, ordering):
    count = ordering.shape[0]
    q_sorted = jnp.take(query, ordering, axis=0).reshape(count // C, C, HD)
    k_sorted = jnp.take(keyed, ordering, axis=0).reshape(count // C, C, HD)
    v_sorted = jnp.take(valued, ordering, axis=0).reshape(count // C, C, HD)
    scores = reduced_restore(jnp.einsum('nqd,nkd->nqk', q_sorted, k_sorted, precision=HIGHEST_ACCURACY) * (1.0 / math.sqrt(HD)))
    top = lax.optimization_barrier(jnp.max(scores, axis=-1, keepdims=True))
    expo = jnp.exp(scores - top)
    probs = reduced_copy(expo / lax.optimization_barrier(jnp.sum(expo, axis=-1, keepdims=True)))
    mixed = jnp.einsum('nqk,nkd->nqd', probs, v_sorted, precision=HIGHEST_ACCURACY).reshape(count, HD)
    return jnp.zeros_like(mixed).at[ordering].set(mixed)

def sequence_attention(packed):
    query, keyed, valued, ordering = packed
    return jax.vmap(head_attention)(query, keyed, valued, ordering)

def forward_group(inputs, qkv_weight, qv_bias, out_weight, out_bias, first_gain, first_shift, first_layer_weight, first_layer_bias, second_layer_weight, second_layer_bias, second_gain, second_shift, ordering):
    group = inputs.shape[1]
    bias_full = jnp.stack([qv_bias[0], jnp.zeros_like(qv_bias[0]), qv_bias[1]])
    qkv = jnp.einsum('lsd,dje->lsje', inputs, qkv_weight, precision=HIGHEST_ACCURACY) + bias_full
    qkv = reduced_copy(reduced_restore(qkv))
    heads_major = qkv.reshape(L, group, 3, H, HD).transpose(1, 2, 3, 0, 4)
    mixed = lax.map(jax.checkpoint(sequence_attention), (heads_major[:, 0], heads_major[:, 1], heads_major[:, 2], ordering))
    mixed = mixed.transpose(2, 0, 1, 3).reshape(L, group, D)
    mixed = reduced_copy(reduced_restore(mixed))
    attended = reduced_restore(jnp.einsum('lse,ed->lsd', mixed, out_weight, precision=HIGHEST_ACCURACY) + out_bias)
    first_normed = layer_norm(inputs + attended, first_gain, first_shift)
    upper_hidden = reduced_restore(jnp.einsum('zvn,nr->zvr', reduced_copy(first_normed), first_layer_weight, precision=HIGHEST_ACCURACY) + first_layer_bias)
    active_tokens = reduced_copy(jax.nn.gelu(upper_hidden, approximate=False))
    lowered_rows = reduced_restore(jnp.einsum('ijg,gk->ijk', active_tokens, second_layer_weight, precision=HIGHEST_ACCURACY) + second_layer_bias)
    return layer_norm(first_normed + lowered_rows, second_gain, second_shift)

def reference(inputs, qkv_weight, qv_bias, out_weight, out_bias, first_gain, first_shift, first_layer_weight, first_layer_bias, second_layer_weight, second_layer_bias, second_gain, second_shift, cluster_order, masked_rows, masked_grad):
    params = tuple((weight.astype(jnp.float32) for weight in (qkv_weight, qv_bias, out_weight, out_bias, first_gain, first_shift, first_layer_weight, first_layer_bias, second_layer_weight, second_layer_bias, second_gain, second_shift)))
    group = math.gcd(SEQS, max(1, 4096 // L))
    blocks = SEQS // group
    grouped = inputs.astype(jnp.float32).reshape(L, blocks, group, D).transpose(1, 0, 2, 3)
    seq_index = jnp.arange(SEQS, dtype=jnp.int32)[:, None]
    dense = jnp.zeros((SEQS, L, D), jnp.float32).at[seq_index, masked_rows].set(masked_grad.astype(jnp.float32))
    dense = dense.reshape(blocks, group, L, D).transpose(0, 2, 1, 3)
    orders = cluster_order.reshape(blocks, group, H, L)

    def step(totals, pieces):
        block_in, block_grad, block_order = pieces

        def forward_here(values, *weights):
            return forward_group(values, *weights, block_order)
        result, pull = jax.vjp(forward_here, block_in, *params)
        grads = pull(block_grad)
        totals = jax.tree.map(jnp.add, totals, tuple(grads[1:]))
        return (totals, (result, grads[0]))
    start = tuple((jnp.zeros_like(weight) for weight in params))
    totals, (results, grad_blocks) = lax.scan(step, start, (grouped, dense, orders))
    outputs = results.transpose(1, 0, 2, 3).reshape(L, SEQS, D).astype(jnp.bfloat16)
    grad_inputs = grad_blocks.transpose(1, 0, 2, 3).reshape(L, SEQS, D)
    return (outputs, grad_inputs, totals[0], totals[1], totals[2], totals[3], totals[4], totals[5], totals[6], totals[7], totals[8], totals[9], totals[10], totals[11])
```

```python
import math

import jax
import jax.numpy as jnp
from jax import lax
from jax.experimental import pallas as pl
from jax.experimental.pallas import tpu as pltpu
from jax.sharding import PartitionSpec as P

HD = 64
C = 128
NORM_EPS = 1e-05
BF = jnp.bfloat16
F32 = jnp.float32
MESH = pl.DeviceIdType.MESH
RSQRT2 = 1.0 / math.sqrt(2.0)
RSQRT2PI = 1.0 / math.sqrt(2.0 * math.pi)

NN = (((1,), (0,)), ((), ()))
NT = (((1,), (1,)), ((), ()))
TN = (((0,), (0,)), ((), ()))


def mm(a, b, dims=NN):
    return lax.dot_general(a, b, dims, preferred_element_type=F32)


def kernel(
    x_in, ord_in, wa_in, wb_in, wc_in, bias_in, par, mr_in, mg_in,
    o1, o2, res, vout,
    xall, ordv, wg, bias, mr, mg, wm, wo, qkv, oc, sq, skv, pr, ms, mix,
    snd, rcv, op, fst, n1, rs1, flow, act, dg, dl, da, dm, g, st1, st2, st3,
    rb, tok, gtok, vb, vr,
    x_s, x_r, x_l, cx_s, cx_r, o_s, o_r, o_l, b_s, b_r, b_l, m_s, m_r, m_l,
    wz_s, wz_s2, wz_r, wx_s, wx_r, w_l, pe_s, pe_r, t_s, t_r, t_l, v_s, v_r,
    g1_s, g1_r, g2_s, g2_r, g3_s, g3_r, ag_s, ag_r, ag_l, ce_s, ce_r,
):
    w_in = (wa_in, wb_in, wc_in)
    d = lax.axis_index("dp")
    z = lax.axis_index("tensor")
    c = lax.rem(d, 2)
    base = d - c
    sib = base + 1 - c
    px = lax.rem(lax.div(d, 2), 2)
    py = lax.rem(lax.div(d, 4), 2)
    xn = d + 2 - 4 * px
    yn = d + 4 - 8 * py
    zc = lax.div(z, 2)
    zj = lax.rem(z, 2)
    up = 1 - 2 * c
    zz = 3 * c + z * up
    prim = zc == c

    def rc(src, dst, ss, rs, dev):
        return pltpu.make_async_remote_copy(
            src_ref=src, dst_ref=dst, send_sem=ss, recv_sem=rs,
            device_id=dev, device_id_type=MESH,
        )

    def wait_send(src, ss):
        rc(src, src, ss, ss, (sib, z)).wait_send()

    def wait_recv(dst, rs):
        rc(dst, dst, rs, rs, (sib, z)).wait_recv()

    def lc(src, dst, sem):
        return pltpu.make_async_copy(src, dst, sem)

    bar = pltpu.get_barrier_semaphore()
    for k in range(1, 8):
        oc_, oz = k % 2, k // 2
        dev = (base + lax.rem(c + oc_, 2), lax.rem(z + oz, 4))
        pl.semaphore_signal(bar, inc=1, device_id=dev, device_id_type=MESH)
    for dev in ((xn, z), (yn, z)):
        pl.semaphore_signal(bar, inc=1, device_id=dev, device_id_type=MESH)
    pl.semaphore_wait(bar, 9)

    def pp(r):
        return (px, py) if r == 0 else (py, px)

    def nbs(r):
        return ((xn, z), (yn, z)) if r == 0 else ((yn, z), (xn, z))

    def blk(r, p1, p2):
        return pl.ds(pl.multiple_of(384 * r + 96 * (2 * p1 + p2), 32), 96)

    def uof(v):
        return c + v * up

    def w_start(a):
        for v in range(2):
            for r in range(2):
                p1, p2 = pp(r)
                rows = blk(r, p1, p2)
                src = w_in[a].at[rows]
                dst = wg.at[a, uof(v), rows]

                @pl.when(zz == v)
                def _(src=src, dst=dst, v=v, r=r):
                    rc(src, dst, wz_s.at[a, v, r], wz_r.at[a, v, r], (d, z + up)).start()
                    if v == 1:
                        rc(src, dst, wz_s2.at[a, r], wz_r.at[a, v, r], (d, z - up)).start()

    def w_local(a):
        for v in range(2):

            @pl.when(zz == v)
            def _(v=v):
                lc(w_in[a], wg.at[a, uof(v)], w_l.at[a]).start()

    def w_fwd(a):
        for v in range(2):
            for r in range(2):
                p1, p2 = pp(r)
                ref = wg.at[a, uof(v), blk(r, p1, p2)]
                n1_, n2_ = nbs(r)

                @pl.when(zz != v)
                def _(ref=ref, v=v, r=r, n1_=n1_, n2_=n2_):
                    wait_recv(ref, wz_r.at[a, v, r])
                    rc(ref, ref, wx_s.at[a, v, r, 0], wx_r.at[a, v, r, 0], n1_).start()
                    rc(ref, ref, wx_s.at[a, v, r, 1], wx_r.at[a, v, r, 1], n2_).start()

                fw = ((zz == 1) | (zz == 2)) if v == 0 else (zz == 2)

                @pl.when(fw)
                def _(ref=ref, v=v, r=r):
                    rc(ref, ref, wz_s.at[a, v, r], wz_r.at[a, v, r], (d, z + up)).start()

    def w_fwd2(a):
        for v in range(2):
            for r in range(2):
                p1, p2 = pp(r)
                ref = wg.at[a, uof(v), blk(r, 1 - p1, p2)]
                n1_, n2_ = nbs(r)

                @pl.when(zz != v)
                def _(ref=ref, v=v, r=r, n2_=n2_):
                    wait_recv(ref, wx_r.at[a, v, r, 0])
                    rc(ref, ref, wx_s.at[a, v, r, 2], wx_r.at[a, v, r, 2], n2_).start()

    def w_done(a):
        for v in range(2):
            for r in range(2):
                p1, p2 = pp(r)

                @pl.when(zz != v)
                def _(v=v, r=r, p1=p1, p2=p2):
                    wait_recv(wg.at[a, uof(v), blk(r, p1, 1 - p2)], wx_r.at[a, v, r, 1])
                    wait_recv(wg.at[a, uof(v), blk(r, 1 - p1, 1 - p2)], wx_r.at[a, v, r, 2])

            @pl.when(zz == v)
            def _(v=v):
                lc(w_in[a], wg.at[a, uof(v)], w_l.at[a]).wait()

    def w_end(a):
        for v in range(2):
            for r in range(2):
                p1, p2 = pp(r)
                rows = blk(r, p1, p2)
                ref = wg.at[a, uof(v), rows]
                sent = (zz <= 2) if v == 0 else ((zz == 1) | (zz == 2))

                @pl.when(sent)
                def _(ref=ref, v=v, r=r):
                    wait_send(ref, wz_s.at[a, v, r])

                if v == 1:

                    @pl.when(zz == 1)
                    def _(ref=ref, r=r):
                        wait_send(ref, wz_s2.at[a, r])

                @pl.when(zz != v)
                def _(ref=ref, v=v, r=r):
                    for k in range(3):
                        wait_send(ref, wx_s.at[a, v, r, k])

    for j in range(2):
        dev = (base + zc, 2 * c + j)
        self_ = (zc == c) & (z == 2 * c + j)

        @pl.when(self_)
        def _(j=j):
            lc(ord_in.at[j], ordv.at[zj], o_l).start()

        @pl.when(jnp.logical_not(self_))
        def _(j=j, dev=dev):
            rc(ord_in.at[j], ordv.at[zj], o_s.at[j], o_r.at[zj], dev).start()

    @pl.when(prim)
    def _():
        for k in range(1, 4):
            dev = (d, lax.rem(z + k, 4))
            rc(bias_in, bias.at[zj], b_s.at[k - 1], b_r.at[zj], dev).start()
        lc(bias_in, bias.at[zj], b_l).start()
        lc(mr_in.at[zj], mr, m_l.at[0]).start()
        lc(mg_in.at[zj], mg, m_l.at[1]).start()
        rc(mr_in.at[zj], mr, m_s.at[0], m_r.at[0], (sib, z)).start()
        rc(mg_in.at[zj], mg, m_s.at[1], m_r.at[1], (sib, z)).start()

    w_start(0)
    w_local(0)

    for j in range(2):
        for h in range(2):
            zt = 2 * c + j
            rows = pl.ds(128 * h, 128)
            self_ = (c == h) & (z == zt)
            src = x_in.at[j, rows]
            dst = xall.at[z, rows]

            @pl.when(self_)
            def _(src=src, dst=dst):
                lc(src, dst, x_l).start()

            @pl.when(jnp.logical_not(self_))
            def _(src=src, dst=dst, j=j, h=h, zt=zt):
                rc(src, dst, x_s.at[j, h], x_r.at[z], (base + h, zt)).start()

    w_local(1)
    w_local(2)
    w_fwd(0)
    w_fwd2(0)
    w_start(1)
    w_start(2)
    crows = pl.ds(pl.multiple_of(128 * c, 128), 128)
    srows = pl.ds(pl.multiple_of(128 * (1 - c), 128), 128)
    for k in range(4):
        ref = xall.at[k, crows]
        loc = prim & (z == k)

        @pl.when(loc)
        def _(ref=ref):
            lc(ref, ref, x_l).wait()

        @pl.when(jnp.logical_not(loc))
        def _(ref=ref, k=k):
            wait_recv(ref, x_r.at[k])

        rc(ref, ref, cx_s.at[k], cx_r.at[k], (sib, z)).start()
    for k in range(4):
        wait_recv(xall.at[k, srows], cx_r.at[k])

    for u in range(2):
        loc = prim & (zj == u)

        @pl.when(loc)
        def _(u=u):
            lc(ord_in.at[0], ordv.at[u], o_l).wait()
            lc(bias_in, bias.at[u], b_l).wait()

        @pl.when(jnp.logical_not(loc))
        def _(u=u):
            wait_recv(ordv.at[u], o_r.at[u])
            wait_recv(bias.at[u], b_r.at[u])

    @pl.when(prim)
    def _():
        lc(mr_in.at[0], mr, m_l.at[0]).wait()
        lc(mg_in.at[0], mg, m_l.at[1]).wait()

    @pl.when(jnp.logical_not(prim))
    def _():
        wait_recv(mr, m_r.at[0])
        wait_recv(mg, m_r.at[1])

    w_done(0)

    lane = lax.broadcasted_iota(jnp.int32, (128, 128), 1)
    sub = lax.broadcasted_iota(jnp.int32, (128, 1024), 0)
    low = lane < 64
    lowb = lax.broadcasted_iota(jnp.int32, (768, 128), 1) < 64

    def pick(m, a, b):
        return jnp.where(m, a.astype(F32), b.astype(F32)).astype(BF)

    wm[:, 0:128] = wg[0, 0, :, 384:512]
    wm[:, 128:256] = pick(lowb, wg[0, 0, :, 640:768], wg[0, 1, :, 640:768])
    wm[:, 256:384] = wg[0, 1, :, 384:512]
    wo[:, 0:128] = wg[0, 0, :, 512:640]
    wo[:, 128:256] = pick(lowb, wg[0, 1, :, 640:768], wg[0, 0, :, 640:768])
    wo[:, 256:384] = wg[0, 1, :, 512:640]
    low1 = lax.broadcasted_iota(jnp.int32, (1, 128), 1) < 64

    def wq(i):
        if i == 1:
            return wm[...]
        return wg[0, i // 2, :, 0:384]

    def bq(i):
        if i == 1:
            return jnp.concatenate(
                [
                    bias[0, 0:1, 384:512],
                    jnp.where(low1, bias[0, 0:1, 640:768], bias[1, 0:1, 640:768]),
                    bias[1, 0:1, 384:512],
                ],
                axis=1,
            )
        return bias[i // 2, 0:1, 0:384]

    def rows_of(m, n):
        return pl.ds(pl.multiple_of(m * n, n), n)

    for i in range(3):
        wv = wq(i)
        bv = bq(i)

        def body(k, _, i=i, wv=wv, bv=bv):
            qkv[i, rows_of(k, 256), :] = (mm(xall[k], wv) + bv).astype(BF)
            return 0

        lax.fori_loop(0, 4, body, 0)

    def columns(h, s):
        row = ordv[h // 3, h % 3 : h % 3 + 1, :]
        oc[s] = jnp.broadcast_to(row, (128, 1024)).T

    def sort_mat(s, r):
        b = oc[s, rows_of(r, 128), :]
        return jnp.concatenate(
            [jnp.where(b == lane + 128 * k, 1.0, 0.0).astype(BF) for k in range(8)], axis=1
        )

    def unsort_mat(h, r):
        row = ordv[h // 3, h % 3 : h % 3 + 1, :]
        return jnp.where(sub + 128 * r == row, 1.0, 0.0).astype(BF)

    def attend(i):
        for s in range(2):
            h = 2 * i + s
            columns(h, s)

            def body(r, _, s=s, h=h):
                got = mm(sort_mat(s, r), qkv[i, :, 128 * s : 128 * s + 256])
                if s == 0:
                    kv = got[:, 0:128].astype(BF)
                    q = jnp.where(low, got[:, 128:256], 0.0).astype(BF)
                else:
                    q = jnp.where(low, 0.0, got[:, 0:128]).astype(BF)
                    kv = got[:, 128:256].astype(BF)
                rr = rows_of(r, 128)
                sq[h, rr, :] = q
                skv[h, rr, :] = kv
                sc = mm(q, kv, NT) * 0.125
                top = jnp.max(sc, axis=-1, keepdims=True)
                ex = jnp.exp(sc - top)
                prob = ex / jnp.sum(ex, axis=-1, keepdims=True)
                pr[h, rr, :] = prob
                mx = mm(prob.astype(BF), kv)
                ms[s, rr, 0:128] = (
                    jnp.where(low, 0.0, mx) if s == 0 else jnp.where(low, mx, 0.0)
                ).astype(BF)
                return 0

            lax.fori_loop(0, 8, body, 0)

        def back(r, _):
            both = mm(unsort_mat(2 * i, r), ms[0, :, 0:128]) + mm(
                unsort_mat(2 * i + 1, r), ms[1, :, 0:128]
            )
            mix[rows_of(r, 128), 128 * i : 128 * i + 128] = both.astype(BF)
            return 0

        lax.fori_loop(0, 8, back, 0)

    attend(0)
    w_fwd(1)
    w_fwd2(1)
    attend(1)
    w_fwd(2)
    w_fwd2(2)
    attend(2)

    mine = 512 * c
    other = 512 - mine

    def at(off, m, n):
        return pl.ds(pl.multiple_of(off + m * n, n), n)

    def partial(fn, k):
        if k >= 2:
            wait_send(snd.at[k % 2], pe_s.at[k - 2])
        for m in range(2):
            snd[k % 2, pl.ds(256 * m, 256), :] = fn(at(other, m, 256)).astype(BF)
        rc(snd.at[k % 2], rcv.at[k], pe_s.at[k], pe_r.at[k], (sib, z)).start()
        for m in range(2):
            op[pl.ds(256 * m, 256), :] = fn(at(mine, m, 256))
        wait_recv(rcv.at[k], pe_r.at[k])

    def share(ref, k):
        own = ref.at[pl.ds(pl.multiple_of(mine, 512), 512)]
        rc(own, own, pe_s.at[4 + k], pe_r.at[4 + k], (sib, z)).start()

    def shared(ref, k):
        wait_recv(ref.at[pl.ds(pl.multiple_of(other, 512), 512)], pe_r.at[4 + k])

    partial(lambda rows: mm(mix[rows, :], wo[...], NT), 0)

    def norm1(m, _):
        rr = rows_of(m, 128)
        v = (
            xall[2 * c + m // 2, pl.ds(pl.multiple_of(128 * lax.rem(m, 2), 128), 128), :].astype(F32)
            + op[rr, :]
            + rcv[0, rr, :].astype(F32)
            + par[0:1, :]
        )
        cen = v - jnp.mean(v, axis=-1, keepdims=True)
        rstd = lax.rsqrt(jnp.mean(cen * cen, axis=-1, keepdims=True) + NORM_EPS)
        nv = cen * rstd
        n1[rr, :] = nv
        rs1[rr, :] = rstd
        fv = nv * par[1:2, :] + par[2:3, :]
        fst[rr, :] = fv
        flow[at(mine, m, 128), :] = fv.astype(BF)
        return 0

    lax.fori_loop(0, 4, norm1, 0)
    share(flow, 0)
    w_done(1)
    w_done(2)

    def ffn_up(off):
        for u in range(2):

            def body(m, _, u=u):
                rr = at(off, m, 128)
                h = mm(flow[rr, :], wg[1, u]) + bias[u, 1:2, :]
                cdf = 0.5 + 0.5 * lax.erf(h * RSQRT2)
                act[rr, 768 * u : 768 * u + 768] = (h * cdf).astype(BF)
                dg[rr, 768 * u : 768 * u + 768] = (
                    cdf + h * (jnp.exp(-0.5 * h * h) * RSQRT2PI)
                ).astype(BF)
                return 0

            lax.fori_loop(0, 4, body, 0)

    ffn_up(mine)
    shared(flow, 0)
    ffn_up(other)
    partial(
        lambda rows: mm(act[rows, 0:768], wg[2, 0]) + mm(act[rows, 768:1536], wg[2, 1]), 1
    )

    vb[0] = jnp.zeros((16, 768), F32)
    ones8 = jnp.zeros((1, 768), F32)

    def norm2(m, carry):
        sgain, sshift, dbias = carry
        rr = rows_of(m, 128)
        v = fst[rr, :] + op[rr, :] + rcv[1, rr, :].astype(F32) + par[3:4, :]
        cen = v - jnp.mean(v, axis=-1, keepdims=True)
        rstd = lax.rsqrt(jnp.mean(cen * cen, axis=-1, keepdims=True) + NORM_EPS)
        nv = cen * rstd
        tok[rr, :] = (nv * par[4:5, :] + par[5:6, :]).astype(BF)
        pos = lax.broadcasted_iota(jnp.int32, (128, 256), 0) + (mine + 128 * m)
        hits = jnp.where(pos == mr[0:1, :], 1.0, 0.0).astype(BF)
        dout = mm(hits, mg[...])
        gg = dout * par[4:5, :]
        d2 = (
            gg
            - jnp.mean(gg, axis=-1, keepdims=True)
            - nv * jnp.mean(gg * nv, axis=-1, keepdims=True)
        ) * rstd
        fst[rr, :] = d2
        dlo = d2.astype(BF)
        dl[at(mine, m, 128), :] = dlo
        return (
            sgain + jnp.sum(dout * nv, axis=0, keepdims=True),
            sshift + jnp.sum(dout, axis=0, keepdims=True),
            dbias + jnp.sum(dlo.astype(F32), axis=0, keepdims=True),
        )

    sg, ss, db = lax.fori_loop(0, 4, norm2, (ones8, ones8, ones8))
    share(dl, 1)
    vb[0, 0:1, :] = sg
    vb[0, 1:2, :] = ss
    vb[0, 2:3, :] = db

    def tok_send(src, dst, k):
        for u in range(2):
            self_ = prim & (z == 2 * c + u)
            s_ = src.at[pl.ds(256 * u, 256)]
            d_ = dst.at[zj]

            @pl.when(self_)
            def _(s_=s_, d_=d_):
                lc(s_, d_, t_l.at[k]).start()

            @pl.when(jnp.logical_not(self_))
            def _(s_=s_, d_=d_, u=u):
                rc(s_, d_, t_s.at[k, u], t_r.at[k, zj], (base + zc, 2 * c + u)).start()

    def tok_wait(src, dst, k):
        for j in range(2):
            loc = prim & (z == 2 * c + j)

            @pl.when(loc)
            def _(j=j):
                lc(src.at[pl.ds(0, 256)], dst.at[j], t_l.at[k]).wait()

            @pl.when(jnp.logical_not(loc))
            def _(j=j):
                wait_recv(dst.at[j], t_r.at[k, j])
                wait_send(src.at[pl.ds(0, 256)], t_s.at[k, j])

    tok_send(tok, o1, 0)

    def g_start(a, u):
        for r in range(2):
            p1, p2 = pp(r)
            src = g.at[a, u, pl.ds(pl.multiple_of(384 * r + 192 * (1 - p1), 64), 192)]
            rc(src, st1.at[a, u, r], g1_s.at[a, u, r], g1_r.at[a, u, r], nbs(r)[0]).start()

    def quarter(ref, r, q):
        return ref.at[pl.ds(pl.multiple_of(96 * q, 32), 96)]

    def g_step2(a, u):
        for r in range(2):
            p1, p2 = pp(r)
            wait_recv(st1.at[a, u, r], g1_r.at[a, u, r])
            rows = blk(r, p1, 1 - p2)
            part = st1[a, u, r, pl.ds(pl.multiple_of(96 * (1 - p2), 32), 96), :]
            g[a, u, rows, :] = (g[a, u, rows, :].astype(F32) + part.astype(F32)).astype(BF)
            rc(
                g.at[a, u, rows], st2.at[a, u, r], g2_s.at[a, u, r], g2_r.at[a, u, r], nbs(r)[1]
            ).start()

    def g_step3(a, u):
        for r in range(2):
            p1, p2 = pp(r)
            wait_recv(st2.at[a, u, r], g2_r.at[a, u, r])
            rows = blk(r, p1, p2)
            part = st1[a, u, r, pl.ds(pl.multiple_of(96 * p2, 32), 96), :]
            tot = (
                g[a, u, rows, :].astype(F32) + part.astype(F32) + st2[a, u, r].astype(F32)
            ).astype(BF)
            self_ = (c == r) & (z == 2 * c + u)

            @pl.when(self_)
            def _(tot=tot):
                st3[a, z] = tot

            @pl.when(jnp.logical_not(self_))
            def _(tot=tot, rows=rows, r=r):
                g[a, u, rows, :] = tot
                rc(
                    g.at[a, u, rows], st3.at[a, z], g3_s.at[a, u, r], g3_r.at[a, z],
                    (base + r, 2 * c + u),
                ).start()

    q1 = px + c * (py - px)
    q2 = py + c * (px - py)
    e1 = (xn + c * (yn - xn), z)
    e2 = (yn + c * (xn - yn), z)

    def own(r, p1, p2):
        return pl.ds(pl.multiple_of(384 * r + 96 * (2 * p1 + p2), 32), 96)

    def g_step4(a):
        for k in range(4):
            loc = prim & (z == k)

            @pl.when(jnp.logical_not(loc))
            def _(k=k):
                wait_recv(st3.at[a, k], g3_r.at[a, k])

        rb[a] = (
            st3[a, 0].astype(F32)
            + st3[a, 1].astype(F32)
            + st3[a, 2].astype(F32)
            + st3[a, 3].astype(F32)
        ).astype(BF)
        dst = res.at[a, own(c, q1, q2)]
        rc(rb.at[a], dst, ag_s.at[a, 0], ag_r.at[a, 0], e1).start()
        rc(rb.at[a], dst, ag_s.at[a, 1], ag_r.at[a, 1], e2).start()
        rc(rb.at[a], dst, ce_s.at[a, 0], ce_r.at[a, 0], (sib, z)).start()
        lc(rb.at[a], dst, ag_l.at[a]).start()

    def g_step5(a):
        ref = res.at[a, own(c, 1 - q1, q2)]
        wait_recv(ref, ag_r.at[a, 0])
        rc(ref, ref, ag_s.at[a, 2], ag_r.at[a, 2], e2).start()
        rc(ref, ref, ce_s.at[a, 1], ce_r.at[a, 1], (sib, z)).start()

    def g_step6(a):
        ref = res.at[a, own(c, q1, 1 - q2)]
        wait_recv(ref, ag_r.at[a, 1])
        rc(ref, ref, ce_s.at[a, 2], ce_r.at[a, 2], (sib, z)).start()
        ref = res.at[a, own(c, 1 - q1, 1 - q2)]
        wait_recv(ref, ag_r.at[a, 2])
        rc(ref, ref, ce_s.at[a, 3], ce_r.at[a, 3], (sib, z)).start()

    def g_end(a):
        lc(rb.at[a], res.at[a, own(c, q1, q2)], ag_l.at[a]).wait()
        o_ = 1 - c
        for k, rows in enumerate(
            (own(o_, q2, q1), own(o_, 1 - q2, q1), own(o_, q2, 1 - q1), own(o_, 1 - q2, 1 - q1))
        ):
            wait_recv(res.at[a, rows], ce_r.at[a, k])
            wait_send(rb.at[a], ce_s.at[a, k])
        for k in range(3):
            wait_send(rb.at[a], ag_s.at[a, k])
        for u in range(2):
            for r in range(2):
                wait_send(st1.at[a, u, r], g1_s.at[a, u, r])
                wait_send(st2.at[a, u, r], g2_s.at[a, u, r])

                @pl.when(jnp.logical_not((c == r) & (z == 2 * c + u)))
                def _(u=u, r=r):
                    wait_send(st2.at[a, u, r], g3_s.at[a, u, r])

    shared(dl, 1)

    def tmm(dst_fn, lhs_fn, rhs_fn, n):
        def body(m, _):
            dst_fn(m, mm(lhs_fn(m), rhs_fn(), TN))
            return 0

        lax.fori_loop(0, n, body, 0)

    for u in range(2):
        for n in range(3):
            cols = slice(768 * u + 256 * n, 768 * u + 256 * n + 256)
            g[2, u, 256 * n : 256 * n + 256, :] = mm(act[:, cols], dl[...], TN).astype(BF)
        g_start(2, u)

    for u in range(2):

        def dup(m, carry, u=u):
            rr = rows_of(m, 128)
            cols = slice(768 * u, 768 * u + 768)
            dv = (mm(dl[rr, :], wg[2, u], NT) * dg[rr, cols].astype(F32)).astype(BF)
            dg[rr, cols] = dv
            return carry + jnp.sum(dv.astype(F32), axis=0, keepdims=True)

        ub = lax.fori_loop(0, 8, dup, jnp.zeros((1, 768), F32))
        vb[0, pl.ds(6 + 2 * c + u, 1), :] = ub
    for u in range(2):
        g_step2(2, u)
    partial(
        lambda rows: mm(dg[rows, 0:768], wg[1, 0], NT) + mm(dg[rows, 768:1536], wg[1, 1], NT), 2
    )
    for u in range(2):
        for n in range(3):
            g[1, u, 256 * n : 256 * n + 256, :] = mm(
                flow[:, 256 * n : 256 * n + 256], dg[:, 768 * u : 768 * u + 768], TN
            ).astype(BF)
        g_start(1, u)
    for u in range(2):
        g_step3(2, u)

    def norm1b(m, carry):
        fg, fs, ob = carry
        rr = rows_of(m, 128)
        df = fst[rr, :] + op[rr, :] + rcv[2, rr, :].astype(F32)
        nv = n1[rr, :]
        gg = df * par[1:2, :]
        dr = (
            gg
            - jnp.mean(gg, axis=-1, keepdims=True)
            - nv * jnp.mean(gg * nv, axis=-1, keepdims=True)
        ) * rs1[rr, :]
        fst[rr, :] = dr
        dlo = dr.astype(BF)
        da[at(mine, m, 128), :] = dlo
        return (
            fg + jnp.sum(df * nv, axis=0, keepdims=True),
            fs + jnp.sum(df, axis=0, keepdims=True),
            ob + jnp.sum(dlo.astype(F32), axis=0, keepdims=True),
        )

    fg, fs, ob = lax.fori_loop(0, 4, norm1b, (ones8, ones8, ones8))
    share(da, 2)
    vb[0, 3:4, :] = fg
    vb[0, 4:5, :] = fs
    vb[0, 5:6, :] = ob
    for u in range(2):
        g_step2(1, u)
    shared(da, 2)

    def dmix(m, _):
        rr = rows_of(m, 256)
        dm[rr, :] = mm(da[rr, :], wo[...]).astype(BF)
        return 0

    lax.fori_loop(0, 4, dmix, 0)
    for n in range(3):
        gw = mm(da[:, 256 * n : 256 * n + 256], mix[...], TN)
        rows = slice(256 * n, 256 * n + 256)
        g[0, 0, rows, 512:640] = gw[:, 0:128].astype(BF)
        g[0, 1, rows, 512:640] = gw[:, 256:384].astype(BF)
        wm_ = gw[:, 128:256].astype(BF)
        g[0, 0, rows, 640:768] = wm_
        g[0, 1, rows, 640:768] = wm_

    def attend_back(i):
        for s in range(2):
            h = 2 * i + s
            columns(h, s)

            def body(r, _, s=s, h=h):
                rr = rows_of(r, 128)
                uu = mm(sort_mat(s, r), dm[:, 128 * i : 128 * i + 128])
                uu = (jnp.where(low, 0.0, uu) if s == 0 else jnp.where(low, uu, 0.0)).astype(BF)
                kv = skv[h, rr, :]
                q = sq[h, rr, :]
                prob = pr[h, rr, :]
                dp = mm(uu, kv, NT)
                cen = jnp.sum(prob * dp, axis=-1, keepdims=True)
                ds = (prob * (dp - cen)).astype(BF)
                dq = mm(ds, kv) * 0.125
                dkv = mm(prob.astype(BF), uu, TN) + mm(ds, q, TN) * 0.125
                if s == 0:
                    ms[s, rr, 0:128] = dkv.astype(BF)
                    ms[s, rr, 128:256] = jnp.where(low, dq, 0.0).astype(BF)
                else:
                    ms[s, rr, 0:128] = jnp.where(low, 0.0, dq).astype(BF)
                    ms[s, rr, 128:256] = dkv.astype(BF)
                return 0

            lax.fori_loop(0, 8, body, 0)

        def back(r, carry):
            ga = mm(unsort_mat(2 * i, r), ms[0])
            gb = mm(unsort_mat(2 * i + 1, r), ms[1])
            out = jnp.concatenate(
                [ga[:, 0:128], ga[:, 128:256] + gb[:, 0:128], gb[:, 128:256]], axis=1
            )
            qkv[i, rows_of(r, 128), :] = out.astype(BF)
            return carry + jnp.sum(out, axis=0, keepdims=True)

        return lax.fori_loop(0, 8, back, jnp.zeros((1, 384), F32))

    def gqkv(i):
        for n in range(3):
            rows = slice(256 * n, 256 * n + 256)
            gw = mm(
                jnp.concatenate([xall[k, :, rows] for k in range(4)], axis=0), qkv[i], TN
            )
            if i != 1:
                g[0, i // 2, rows, 0:384] = gw.astype(BF)
            else:
                g[0, 0, rows, 384:512] = gw[:, 0:128].astype(BF)
                g[0, 1, rows, 384:512] = gw[:, 256:384].astype(BF)
                lo = low1
                t0 = g[0, 0, rows, 640:768].astype(F32)
                g[0, 0, rows, 640:768] = jnp.where(lo, gw[:, 128:256], t0).astype(BF)
                g[0, 1, rows, 640:768] = jnp.where(lo, t0, gw[:, 128:256]).astype(BF)

    b0 = attend_back(0)
    gqkv(0)
    for u in range(2):
        g_step3(1, u)
    b1 = attend_back(1)
    gqkv(1)
    g_step4(2)
    g_start(0, 0)
    b2 = attend_back(2)
    gqkv(2)
    g_start(0, 1)
    zero = jnp.zeros((1, 128), F32)
    vb[0, pl.ds(10 + 2 * c, 1), :] = jnp.concatenate([b0, b1[:, 0:128], zero, b1[:, 128:256]], axis=1)
    vb[0, pl.ds(11 + 2 * c, 1), :] = jnp.concatenate(
        [b2, b1[:, 256:384], zero, b1[:, 128:256]], axis=1
    )

    vdev = (
        (sib, z), (xn, z), (yn, z), (d, z + 1 - 2 * zj), (d, z + 2 - 4 * zc),
    )

    def v_send(k):
        rc(vb.at[k], vr.at[k], v_s.at[k], v_r.at[k], vdev[k]).start()

    def v_add(k):
        wait_recv(vr.at[k], v_r.at[k])
        vb[k + 1] = vb[k] + vr[k]

    v_send(0)
    partial(
        lambda rows: mm(qkv[0, rows, :], wq(0), NT)
        + mm(qkv[1, rows, :], wq(1), NT)
        + mm(qkv[2, rows, :], wq(2), NT),
        3,
    )

    def gin(m, _):
        rr = rows_of(m, 128)
        gtok[rr, :] = (fst[rr, :] + op[rr, :] + rcv[3, rr, :].astype(F32)).astype(BF)
        return 0

    lax.fori_loop(0, 4, gin, 0)
    tok_send(gtok, o2, 1)
    g_step5(2)
    g_step4(1)
    v_add(0)
    v_send(1)
    g_step2(0, 0)
    g_step2(0, 1)
    g_step6(2)
    g_step5(1)
    v_add(1)
    v_send(2)
    g_step6(1)
    g_step3(0, 0)
    g_step3(0, 1)
    v_add(2)
    v_send(3)
    g_step4(0)
    v_add(3)
    v_send(4)
    g_step5(0)
    v_add(4)
    vout[...] = vb[5]
    g_step6(0)
    for a in range(3):
        g_end(a)
    tok_wait(tok, o1, 0)
    tok_wait(gtok, o2, 1)

    for a in range(3):
        w_end(a)
    for k in range(4):
        wait_send(xall.at[k, crows], cx_s.at[k])
        if k >= 2:
            wait_send(rcv.at[k], pe_s.at[k])
    for k in range(3):
        wait_send(flow.at[pl.ds(0, 512)], pe_s.at[4 + k])
    for k in range(5):
        wait_send(vb.at[k], v_s.at[k])
    for j in range(2):

        @pl.when(jnp.logical_not(prim & (z == 2 * c + j)))
        def _(j=j):
            wait_send(ord_in.at[j], o_s.at[j])

        for h in range(2):

            @pl.when(jnp.logical_not((c == h) & (z == 2 * c + j)))
            def _(j=j, h=h):
                wait_send(x_in.at[j, pl.ds(0, 128)], x_s.at[j, h])

    @pl.when(prim)
    def _():
        for k in range(3):
            wait_send(bias_in, b_s.at[k])
        wait_send(mr_in.at[0], m_s.at[0])
        wait_send(mg_in.at[0], m_s.at[1])


def layer(x, order, wa, wb, wc, bias, par, mr, mg):
    dma = pltpu.SemaphoreType.DMA
    hbm = pl.BlockSpec(memory_space=pl.ANY)
    vmem = pl.BlockSpec(memory_space=pltpu.VMEM)
    V = pltpu.VMEM
    return pl.pallas_call(
        kernel,
        out_shape=(
            jax.ShapeDtypeStruct((2, 256, 768), BF),
            jax.ShapeDtypeStruct((2, 256, 768), BF),
            jax.ShapeDtypeStruct((3, 768, 768), BF),
            jax.ShapeDtypeStruct((16, 768), F32),
        ),
        in_specs=[hbm, hbm, hbm, hbm, hbm, hbm, vmem, hbm, hbm],
        out_specs=(hbm, hbm, hbm, vmem),
        scratch_shapes=[
            V((4, 256, 768), BF),
            V((2, 8, 1024), jnp.int32),
            V((3, 2, 768, 768), BF),
            V((2, 8, 768), F32),
            V((8, 256), jnp.int32),
            V((256, 768), BF),
            V((768, 384), BF),
            V((768, 384), BF),
            V((3, 1024, 384), BF),
            V((2, 1024, 128), jnp.int32),
            V((6, 1024, 128), BF),
            V((6, 1024, 128), BF),
            V((6, 1024, 128), F32),
            V((2, 1024, 256), BF),
            V((1024, 384), BF),
            V((2, 512, 768), BF),
            V((4, 512, 768), BF),
            V((512, 768), F32),
            V((512, 768), F32),
            V((512, 768), F32),
            V((512, 1), F32),
            V((1024, 768), BF),
            V((1024, 1536), BF),
            V((1024, 1536), BF),
            V((1024, 768), BF),
            V((1024, 768), BF),
            V((1024, 384), BF),
            V((3, 2, 768, 768), BF),
            V((3, 2, 2, 192, 768), BF),
            V((3, 2, 2, 96, 768), BF),
            V((3, 4, 96, 768), BF),
            V((3, 96, 768), BF),
            V((512, 768), BF),
            V((512, 768), BF),
            V((6, 16, 768), F32),
            V((5, 16, 768), F32),
            dma((2, 2)), dma((4,)), dma, dma((4,)), dma((4,)),
            dma((2,)), dma((2,)), dma,
            dma((3,)), dma((2,)), dma,
            dma((2,)), dma((2,)), dma((2,)),
            dma((3, 2, 2)), dma((3, 2)), dma((3, 2, 2)),
            dma((3, 2, 2, 3)), dma((3, 2, 2, 3)), dma((3,)),
            dma((7,)), dma((7,)),
            dma((2, 2)), dma((2, 2)), dma((2,)),
            dma((5,)), dma((5,)),
            dma((3, 2, 2)), dma((3, 2, 2)), dma((3, 2, 2)), dma((3, 2, 2)),
            dma((3, 2, 2)), dma((3, 4)), dma((3, 3)), dma((3, 3)), dma((3,)),
            dma((3, 4)), dma((3, 4)),
        ],
        compiler_params=pltpu.CompilerParams(
            collective_id=0, has_side_effects=True, vmem_limit_bytes=60 * 2**20
        ),
    )(x, order, wa, wb, wc, bias, par, mr, mg)


def split64(a, n):
    return [a[..., 64 * k : 64 * k + 64] for k in range(n)]


def shards(
    inputs, qkv_weight, qv_bias, out_weight, out_bias, first_gain, first_shift,
    first_layer_weight, first_layer_bias, second_layer_weight, second_layer_bias,
    second_gain, second_shift, cluster_order, masked_rows, masked_grad,
):
    t = lax.axis_index("tensor")
    even = lax.rem(t, 2) == 0

    q = split64(qkv_weight[:, 0], 3)
    k = split64(qkv_weight[:, 1], 3)
    v = split64(qkv_weight[:, 2], 3)
    o = split64(out_weight.T, 3)

    def arrange(q, k, v, o):
        ev = [k[0], v[0], q[0], q[1], v[1], k[1], k[2], v[2], o[1], o[0], q[2], o[2]]
        od = [k[1], v[1], q[1], q[2], v[2], k[2], v[0], k[0], o[2], o[1], o[0], q[0]]
        return jnp.where(even, jnp.concatenate(ev, axis=-1), jnp.concatenate(od, axis=-1))

    wa = arrange(q, k, v, o)
    zs = [jnp.zeros((64,), BF)] * 3
    bias_a = arrange(split64(qv_bias[0], 3), zs, split64(qv_bias[1], 3), zs)
    bias = jnp.zeros((8, 768), F32).at[0].set(bias_a.astype(F32)).at[1].set(
        first_layer_bias.astype(F32)
    )
    nil = jnp.zeros((768,), BF)
    par = jnp.stack(
        [out_bias, first_gain, first_shift, second_layer_bias, second_gain, second_shift, nil, nil]
    ).astype(F32)
    order = jnp.pad(cluster_order, ((0, 0), (0, 5), (0, 0)))
    masked = masked_rows.shape[1]
    mr = jnp.pad(masked_rows, ((0, 0), (0, 256 - masked)), constant_values=-1)
    mr = jnp.broadcast_to(mr[:, None, :], (2, 8, 256))
    mg = jnp.pad(masked_grad, ((0, 0), (0, 256 - masked), (0, 0)))
    x = inputs.transpose(1, 0, 2)

    o1, o2, res, vec = layer(
        x, order, wa, first_layer_weight, second_layer_weight, bias, par, mr, mg
    )

    many = lax.axis_size("dp") // 8
    if many > 1:
        groups = [[8 * i + j for i in range(many)] for j in range(8)]
        res = lax.psum(res.astype(F32), "dp", axis_index_groups=groups)
        vec = lax.psum(vec, "dp", axis_index_groups=groups)
    res = res.astype(F32)
    outputs = o1.transpose(1, 0, 2)
    grad_inputs = o2.transpose(1, 0, 2).astype(F32)

    def restore(a):
        b = split64(a, 12)
        ev = [b[2], b[3], b[10], b[0], b[5], b[6], b[1], b[4], b[7], b[9], b[8], b[11]]
        od = [b[11], b[2], b[3], b[7], b[0], b[5], b[6], b[1], b[4], b[10], b[9], b[8]]
        both = jnp.where(even, jnp.concatenate(ev, axis=-1), jnp.concatenate(od, axis=-1))
        return both[..., 0:576], both[..., 576:768]

    gq, go = restore(res[0])
    row = lax.dynamic_slice_in_dim(vec, 10 + t, 1, 0)
    gb = restore(row)[0].reshape(3, 192)
    return (
        outputs,
        grad_inputs,
        gq.reshape(768, 3, 192),
        jnp.stack([gb[0], gb[2]]),
        go.T,
        vec[5],
        vec[3],
        vec[4],
        res[1],
        lax.dynamic_slice_in_dim(vec, 6 + t, 1, 0)[0],
        res[2],
        vec[2],
        vec[0],
        vec[1],
    )


def solution(mesh):
    placed = (
        P("tensor", "dp", None), P(None, None, "tensor"), P(None, "tensor"), P("tensor", None),
        P(), P(), P(), P(None, "tensor"), P("tensor"), P("tensor", None), P(), P(), P(),
        P("dp", "tensor", None), P("dp", None), P("dp", None, None),
    )
    return jax.shard_map(
        shards,
        mesh=mesh,
        in_specs=placed,
        out_specs=(
            P("tensor", "dp", None), P("tensor", "dp", None), P(None, None, "tensor"),
            P(None, "tensor"), P("tensor", None), P(), P(), P(), P(None, "tensor"), P("tensor"),
            P("tensor", None), P(), P(), P(),
        ),
        check_vma=False,
    )
```

```python
import math

import jax
import jax.numpy as jnp
from jax import lax
from jax.experimental import pallas as pl
from jax.experimental.pallas import tpu as pltpu
from jax.sharding import PartitionSpec as P

HD = 64
C = 128
NORM_EPS = 1e-05
BF = jnp.bfloat16
F32 = jnp.float32
MESH = pl.DeviceIdType.MESH
RSQRT2 = 1.0 / math.sqrt(2.0)
RSQRT2PI = 1.0 / math.sqrt(2.0 * math.pi)

NN = (((1,), (0,)), ((), ()))
NT = (((1,), (1,)), ((), ()))
TN = (((0,), (0,)), ((), ()))


def mm(a, b, dims=NN):
    return lax.dot_general(a, b, dims, preferred_element_type=F32)


def kernel(
    x_in, ord_in, wq_in, wo_in, wb_in, wc_in, mr_in, mg_in, qb_in,
    p0, p1_, p2_, p3_, p4_, p5_, p6_,
    o1, o2, ra, rbb, rcc, vout,
    xall, x3, ordv, wg, bias, bias_in, par, mr, mg3, mg, wq, wo, qkv, oc, sq, skv, pr, mix,
    snd, rcv, op, fst, n1, rs1, flow, act, dg, dl, g, st1, st2, st3,
    rb, vb, vr,
    x_s, x_r, x_l, cx_s, cx_r, o_s, o_r, o_l, b_s, b_r, b_l, m_s, m_r, m_l,
    wz_s, wz_s2, wz_r, wx_s, wx_r, w_l, pe_s, pe_r, t_s, t_r, t_l, v_s, v_r,
    g1_s, g1_r, g2_s, g2_r, g3_s, g3_r, ag_s, ag_r, ag_l, ce_s, ce_r,
):
    w_in = (None, wb_in, wc_in)
    res = (ra, rbb, rcc)
    dm = act.at[:, 0:384]
    ms = (act.at[:, 512:768], act.at[:, 768:1024])
    tok = wg.at[0, 0, pl.ds(0, 512)]
    gtok = wg.at[0, 1, pl.ds(0, 512)]
    d = lax.axis_index("dp")
    z = lax.axis_index("tensor")
    c = lax.rem(d, 2)
    base = d - c
    sib = base + 1 - c
    px = lax.rem(lax.div(d, 2), 2)
    py = lax.rem(lax.div(d, 4), 2)
    xn = d + 2 - 4 * px
    yn = d + 4 - 8 * py
    zc = lax.div(z, 2)
    zj = lax.rem(z, 2)
    up = 1 - 2 * c
    zz = 3 * c + z * up
    prim = zc == c

    def rc(src, dst, ss, rs, dev):
        return pltpu.make_async_remote_copy(
            src_ref=src, dst_ref=dst, send_sem=ss, recv_sem=rs,
            device_id=dev, device_id_type=MESH,
        )

    def wait_send(src, ss):
        rc(src, src, ss, ss, (sib, z)).wait_send()

    def wait_recv(dst, rs):
        rc(dst, dst, rs, rs, (sib, z)).wait_recv()

    def lc(src, dst, sem):
        return pltpu.make_async_copy(src, dst, sem)

    bar = pltpu.get_barrier_semaphore()
    for k in range(1, 8):
        oc_, oz = k % 2, k // 2
        dev = (base + lax.rem(c + oc_, 2), lax.rem(z + oz, 4))
        pl.semaphore_signal(bar, inc=1, device_id=dev, device_id_type=MESH)
    for dev in ((xn, z), (yn, z)):
        pl.semaphore_signal(bar, inc=1, device_id=dev, device_id_type=MESH)
    pl.semaphore_wait(bar, 9)

    def pp(r):
        return (px, py) if r == 0 else (py, px)

    def nbs(r):
        return ((xn, z), (yn, z)) if r == 0 else ((yn, z), (xn, z))

    def blk(r, p1, p2):
        return pl.ds(pl.multiple_of(384 * r + 96 * (2 * p1 + p2), 32), 96)

    def uof(v):
        return c + v * up

    def w_start(a):
        for v in range(2):
            for r in range(2):
                p1, p2 = pp(r)
                rows = blk(r, p1, p2)
                dst = wg.at[a, uof(v), rows]
                if a > 0:
                    parts = ((zz == v, w_in[a].at[rows]),)
                elif r == 0:
                    parts = ((zz == v, wq_in.at[rows]),)
                else:
                    off = pl.ds(pl.multiple_of(96 * p2, 32), 96)
                    high = pl.ds(pl.multiple_of(384 + 96 * p2, 32), 96)
                    parts = (
                        ((zz == v) & (p1 == 0), wq_in.at[high]),
                        ((zz == v) & (p1 == 1), wo_in.at[off]),
                    )
                near = z + up if v == 0 else z - up
                far = z + 2 * up if v == 0 else z + up
                for cond, src in parts:

                    @pl.when(cond)
                    def _(src=src, dst=dst, v=v, r=r, near=near, far=far):
                        rc(src, dst, wz_s.at[a, v, r], wz_r.at[a, v, r], (d, near)).start()
                        rc(src, dst, wz_s2.at[a, v, r], wz_r.at[a, v, r], (d, far)).start()

    def w_copies(a, v):
        if a > 0:
            return (lc(w_in[a], wg.at[a, uof(v)], w_l.at[a]),)
        return (
            lc(wq_in, wg.at[0, uof(v), pl.ds(0, 576)], w_l.at[0]),
            lc(wo_in, wg.at[0, uof(v), pl.ds(576, 192)], w_l.at[3]),
        )

    def w_local(a):
        for v in range(2):

            @pl.when(zz == v)
            def _(v=v):
                for cp in w_copies(a, v):
                    cp.start()

    def w_fwd(a, stage):
        for v in range(2):
            for r in range(2):
                p1, p2 = pp(r)
                ref = wg.at[a, uof(v), blk(r, p1, p2)]
                n1_, n2_ = nbs(r)
                cond = (zz == 3) if stage else ((zz == 1 - v) | (zz == 2))

                @pl.when(cond)
                def _(ref=ref, v=v, r=r, n1_=n1_, n2_=n2_):
                    wait_recv(ref, wz_r.at[a, v, r])
                    rc(ref, ref, wx_s.at[a, v, r, 0], wx_r.at[a, v, r, 0], n1_).start()
                    rc(ref, ref, wx_s.at[a, v, r, 1], wx_r.at[a, v, r, 1], n2_).start()

                if not stage:

                    @pl.when(zz == 2)
                    def _(ref=ref, v=v, r=r):
                        rc(ref, ref, wz_s.at[a, v, r], wz_r.at[a, v, r], (d, z + up)).start()

    def w_fwd2(a):
        for v in range(2):
            for r in range(2):
                p1, p2 = pp(r)
                ref = wg.at[a, uof(v), blk(r, 1 - p1, p2)]
                n1_, n2_ = nbs(r)

                @pl.when(zz != v)
                def _(ref=ref, v=v, r=r, n2_=n2_):
                    wait_recv(ref, wx_r.at[a, v, r, 0])
                    rc(ref, ref, wx_s.at[a, v, r, 2], wx_r.at[a, v, r, 2], n2_).start()

    def w_done(a):
        for v in range(2):
            for r in range(2):
                p1, p2 = pp(r)

                @pl.when(zz != v)
                def _(v=v, r=r, p1=p1, p2=p2):
                    wait_recv(wg.at[a, uof(v), blk(r, p1, 1 - p2)], wx_r.at[a, v, r, 1])
                    wait_recv(wg.at[a, uof(v), blk(r, 1 - p1, 1 - p2)], wx_r.at[a, v, r, 2])

            @pl.when(zz == v)
            def _(v=v):
                for cp in w_copies(a, v):
                    cp.wait()

    def w_end(a):
        for v in range(2):
            for r in range(2):
                p1, p2 = pp(r)
                ref = wg.at[a, uof(v), blk(r, p1, p2)]

                @pl.when((zz == v) | (zz == 2))
                def _(ref=ref, v=v, r=r):
                    wait_send(ref, wz_s.at[a, v, r])

                @pl.when(zz == v)
                def _(ref=ref, v=v, r=r):
                    wait_send(ref, wz_s2.at[a, v, r])

                @pl.when(zz != v)
                def _(ref=ref, v=v, r=r):
                    for k in range(3):
                        wait_send(ref, wx_s.at[a, v, r, k])

    w_start(0)
    w_local(0)
    lc(x_in, x3, x_l).start()
    for k, ref in enumerate((p0, p1_, p2_, p3_, p4_, p5_)):
        par[k : k + 1, :] = ref[...].astype(F32).reshape(1, 768)
    bias_in[...] = jnp.zeros((8, 768), F32)
    bias_in[0:2, 0:192] = qb_in[...].astype(F32)
    bias_in[2:3, :] = p6_[...].astype(F32).reshape(1, 768)

    for j in range(2):
        dev = (base + zc, 2 * c + j)
        self_ = (zc == c) & (z == 2 * c + j)

        @pl.when(self_)
        def _(j=j):
            lc(ord_in, ordv.at[zj], o_l).start()

        @pl.when(jnp.logical_not(self_))
        def _(j=j, dev=dev):
            rc(ord_in, ordv.at[lax.rem(z, 2)], o_s.at[j], o_r.at[zj], dev).start()

    @pl.when(prim)
    def _():
        for k in range(1, 4):
            dev = (d, lax.rem(z + k, 4))
            rc(bias_in, bias.at[zj], b_s.at[k - 1], b_r.at[zj], dev).start()
        lc(bias_in, bias.at[zj], b_l).start()
        lc(mr_in, mr, m_l.at[0]).start()
        lc(mg_in, mg3, m_l.at[1]).start()
        rc(mr_in, mr, m_s.at[0], m_r.at[0], (sib, z)).start()
        rc(mg_in, mg3, m_s.at[1], m_r.at[1], (sib, z)).start()


    w_local(1)
    w_local(2)
    lc(x_in, x3, x_l).wait()

    def part(k, _):
        both = x3[pl.ds(pl.multiple_of(32 * k, 32), 32)].astype(F32)
        for j in range(2):
            dg[pl.ds(pl.multiple_of(256 * j + 32 * k, 32), 32), 0:768] = both[:, j, :].astype(BF)
        return 0

    lax.fori_loop(0, 8, part, 0)
    w_fwd(0, 0)
    w_fwd(0, 1)

    for j in range(2):
        for h in range(2):
            zt = 2 * c + j
            rows = pl.ds(128 * h, 128)
            self_ = (c == h) & (z == zt)
            src = dg.at[pl.ds(256 * j + 128 * h, 128), 0:768]
            dst = xall.at[pl.ds(pl.multiple_of(256 * z + 128 * h, 128), 128)]

            @pl.when(self_)
            def _(src=src, dst=dst):
                lc(src, dst, x_l).start()

            @pl.when(jnp.logical_not(self_))
            def _(src=src, dst=dst, j=j, h=h, zt=zt):
                rc(src, dst, x_s.at[j, h], x_r.at[z], (base + h, zt)).start()

    w_fwd2(0)

    def xrows(k, h):
        return xall.at[pl.ds(pl.multiple_of(256 * k + 128 * h, 128), 128)]

    for k in range(4):
        ref = xrows(k, c)
        loc = prim & (z == k)

        @pl.when(loc)
        def _(ref=ref):
            lc(ref, ref, x_l).wait()

        @pl.when(jnp.logical_not(loc))
        def _(ref=ref, k=k):
            wait_recv(ref, x_r.at[k])

        rc(ref, ref, cx_s.at[k], cx_r.at[k], (sib, z)).start()
    w_start(1)
    for k in range(4):
        wait_recv(xrows(k, 1 - c), cx_r.at[k])

    for u in range(2):
        loc = prim & (zj == u)

        @pl.when(loc)
        def _(u=u):
            lc(ord_in, ordv.at[u], o_l).wait()
            lc(bias_in, bias.at[u], b_l).wait()

        @pl.when(jnp.logical_not(loc))
        def _(u=u):
            wait_recv(ordv.at[u], o_r.at[u])
            wait_recv(bias.at[u], b_r.at[u])

    @pl.when(prim)
    def _():
        lc(mr_in, mr, m_l.at[0]).wait()
        lc(mg_in, mg3, m_l.at[1]).wait()

    @pl.when(jnp.logical_not(prim))
    def _():
        wait_recv(mr, m_r.at[0])
        wait_recv(mg3, m_r.at[1])

    both = mg3[...].astype(F32)
    mg[...] = jnp.where(zj == 0, both[:, 0, :], both[:, 1, :]).astype(BF)
    w_done(0)

    lane = lax.broadcasted_iota(jnp.int32, (512, 128), 1)
    sub = lax.broadcasted_iota(jnp.int32, (512, 1024), 0)
    low = lane < 64

    def place(h, kind):
        return h // 3, slice(192 * kind + 64 * (h % 3), 192 * kind + 64 * (h % 3) + 64)

    def pair_rows(i):
        a, b = 2 * i, 2 * i + 1
        return (place(a, 1), place(a, 2), place(a, 0), place(b, 0), place(b, 2), place(b, 1))

    for i in range(3):
        for n, (u, rows) in enumerate(pair_rows(i)):
            wq[384 * i + 64 * n : 384 * i + 64 * n + 64, :] = wg[0, u, rows, :]
        for n, (u, rows) in enumerate((place(2 * i + 1, 3), place(2 * i, 3))):
            wo[128 * i + 64 * n : 128 * i + 64 * n + 64, :] = wg[0, u, rows, :]

    def bq(i):
        nil = jnp.zeros((1, 64), F32)

        def take(h, row):
            return bias[h // 3, row : row + 1, 64 * (h % 3) : 64 * (h % 3) + 64]

        a, b = 2 * i, 2 * i + 1
        return jnp.concatenate(
            [nil, take(a, 1), take(a, 0), take(b, 0), take(b, 1), nil], axis=1
        )

    def rows_of(m, n):
        return pl.ds(pl.multiple_of(m * n, n), n)

    for lo_, hi_ in ((0, 2), (2, 3)):
        bv = jnp.concatenate([bq(i) for i in range(lo_, hi_)], axis=1)
        cols = slice(384 * lo_, 384 * hi_)

        def body(k, _, cols=cols, bv=bv):
            rr = rows_of(k, 512)
            qkv[rr, cols] = (mm(xall[rr, :], wq[cols, :], NT) + bv).astype(BF)
            return 0

        lax.fori_loop(0, 2, body, 0)

    w_start(2)

    def columns(h, s):
        row = ordv[h // 3, h % 3, pl.ds(zj, 1), :]
        oc[s] = jnp.broadcast_to(row, (128, 1024)).T

    def sort_mat(s, t):
        b = oc[s, rows_of(t, 512), :]
        return jnp.concatenate(
            [jnp.where(b == lane + 128 * k, 1.0, 0.0).astype(BF) for k in range(8)], axis=1
        )

    def unsort_mat(h, t):
        row = ordv[h // 3, h % 3, pl.ds(zj, 1), :]
        return jnp.where(sub + 512 * t == row, 1.0, 0.0).astype(BF)

    four = range(4)

    def piece(w, k):
        return w[128 * k : 128 * k + 128]

    def attend(i):
        for s in range(2):
            columns(2 * i + s, s)

        def body(t, _):
            rr = rows_of(t, 512)
            q, kv = [], []
            for s in range(2):
                at_ = 384 * i + 128 * s
                w = mm(sort_mat(s, t), qkv[:, at_ : at_ + 256])
                if s == 0:
                    kv.append(w[:, 0:128].astype(BF))
                    q.append((jnp.where(low, w[:, 128:256], 0.0) * 0.125).astype(BF))
                else:
                    q.append((jnp.where(low, 0.0, w[:, 0:128]) * 0.125).astype(BF))
                    kv.append(w[:, 128:256].astype(BF))
                sq[2 * i + s, rr, :] = q[s]
                skv[2 * i + s, rr, :] = kv[s]
            for s in range(2):
                sc = [mm(piece(q[s], k), piece(kv[s], k), NT) for k in four]
                sc = jnp.concatenate(sc, axis=0)
                ex = jnp.exp(sc - jnp.max(sc, axis=-1, keepdims=True))
                prob = ex * (1.0 / jnp.sum(ex, axis=-1, keepdims=True))
                pr[2 * i + s, rr, :] = prob
                pb = prob.astype(BF)
                mx = jnp.concatenate([mm(piece(pb, k), piece(kv[s], k)) for k in four], axis=0)
                keep = jnp.where(low, 0.0, mx) if s == 0 else jnp.where(low, mx, 0.0)
                ms[s][rr, 0:128] = keep.astype(BF)
            return 0

        lax.fori_loop(0, 2, body, 0)

        def back(t, _):
            both = mm(unsort_mat(2 * i, t), ms[0][:, 0:128]) + mm(
                unsort_mat(2 * i + 1, t), ms[1][:, 0:128]
            )
            mix[rows_of(t, 512), 128 * i : 128 * i + 128] = both.astype(BF)
            return 0

        lax.fori_loop(0, 2, back, 0)

    attend(0)
    w_fwd(1, 0)
    attend(1)
    w_fwd(1, 1)
    w_fwd2(1)
    attend(2)
    w_fwd(2, 0)

    mine = 512 * c
    other = 512 - mine

    def at(off, m, n):
        return pl.ds(pl.multiple_of(off + m * n, n), n)

    def partial(fn, k):
        if k >= 2:
            wait_send(snd.at[k % 2], pe_s.at[k - 2])
        for n in range(3):
            cols = slice(256 * n, 256 * n + 256)
            snd[k % 2, :, cols] = fn(at(other, 0, 512), cols).astype(BF)
        rc(snd.at[k % 2], rcv.at[k], pe_s.at[k], pe_r.at[k], (sib, z)).start()
        for n in range(3):
            cols = slice(256 * n, 256 * n + 256)
            op[:, cols] = fn(at(mine, 0, 512), cols)
        wait_recv(rcv.at[k], pe_r.at[k])

    def share(ref, k):
        own = ref.at[pl.ds(pl.multiple_of(mine, 512), 512)]
        rc(own, own, pe_s.at[4 + k], pe_r.at[4 + k], (sib, z)).start()

    def shared(ref, k):
        wait_recv(ref.at[pl.ds(pl.multiple_of(other, 512), 512)], pe_r.at[4 + k])

    partial(lambda rows, cols: mm(mix[rows, :], wo[:, cols]), 0)

    def norm1(m, _):
        rr = rows_of(m, 128)
        v = (
            xall[at(mine, m, 128), :].astype(F32)
            + op[rr, :]
            + rcv[0, rr, :].astype(F32)
            + par[0:1, :]
        )
        cen = v - jnp.mean(v, axis=-1, keepdims=True)
        rstd = lax.rsqrt(jnp.mean(cen * cen, axis=-1, keepdims=True) + NORM_EPS)
        nv = cen * rstd
        n1[rr, :] = nv
        rs1[rr, :] = rstd
        fv = nv * par[1:2, :] + par[2:3, :]
        fst[rr, :] = fv
        flow[at(mine, m, 128), :] = fv.astype(BF)
        return 0

    lax.fori_loop(0, 4, norm1, 0)
    share(flow, 0)
    w_fwd(2, 1)
    w_done(1)

    for j in range(2):
        for h in range(2):

            @pl.when(jnp.logical_not((c == h) & (z == 2 * c + j)))
            def _(j=j, h=h):
                wait_send(dg.at[pl.ds(0, 128), 0:768], x_s.at[j, h])

    def hidden(t):
        return lax.div(t, 3), rows_of(lax.rem(t, 3), 256)

    def ffn_up(off):
        def body(t, _):
            u, cols = hidden(t)
            rr = at(off, 0, 512)
            h = mm(flow[rr, :], wg[1, u, :, cols]) + bias[u, 2:3, cols]
            cdf = 0.5 + 0.5 * lax.erf(h * RSQRT2)
            act[rr, rows_of(t, 256)] = (h * cdf).astype(BF)
            dg[rr, rows_of(t, 256)] = (cdf + h * (jnp.exp(-0.5 * h * h) * RSQRT2PI)).astype(BF)
            return 0

        lax.fori_loop(0, 6, body, 0)

    ffn_up(mine)
    w_fwd2(2)
    shared(flow, 0)
    ffn_up(other)
    w_done(2)
    partial(
        lambda rows, cols: mm(act[rows, 0:768], wg[2, 0, :, cols])
        + mm(act[rows, 768:1536], wg[2, 1, :, cols]),
        1,
    )

    w_end(0)

    vb[0] = jnp.zeros((16, 768), F32)
    ones8 = jnp.zeros((1, 768), F32)

    def norm2(m, carry):
        sgain, sshift, dbias = carry
        rr = rows_of(m, 128)
        v = fst[rr, :] + op[rr, :] + rcv[1, rr, :].astype(F32) + par[3:4, :]
        cen = v - jnp.mean(v, axis=-1, keepdims=True)
        rstd = lax.rsqrt(jnp.mean(cen * cen, axis=-1, keepdims=True) + NORM_EPS)
        nv = cen * rstd
        tok[rr, :] = (nv * par[4:5, :] + par[5:6, :]).astype(BF)
        pos = lax.broadcasted_iota(jnp.int32, (128, mr.shape[1]), 0) + (mine + 128 * m)
        hits = jnp.where(pos == mr[pl.ds(zj, 1), :], 1.0, 0.0).astype(BF)
        dout = mm(hits, mg[...])
        gg = dout * par[4:5, :]
        d2 = (
            gg
            - jnp.mean(gg, axis=-1, keepdims=True)
            - nv * jnp.mean(gg * nv, axis=-1, keepdims=True)
        ) * rstd
        fst[rr, :] = d2
        dlo = d2.astype(BF)
        dl[at(mine, m, 128), :] = dlo
        return (
            sgain + jnp.sum(dout * nv, axis=0, keepdims=True),
            sshift + jnp.sum(dout, axis=0, keepdims=True),
            dbias + jnp.sum(dlo.astype(F32), axis=0, keepdims=True),
        )

    sg, ss, db = lax.fori_loop(0, 4, norm2, (ones8, ones8, ones8))
    share(dl, 1)
    vb[0, 0:1, :] = sg
    vb[0, 1:2, :] = ss
    vb[0, 2:3, :] = db

    def tok_send(src, dst, k):
        for u in range(2):
            self_ = prim & (z == 2 * c + u)
            s_ = src.at[pl.ds(256 * u, 256)]
            d_ = dst.at[zj]

            @pl.when(self_)
            def _(s_=s_, d_=d_):
                lc(s_, d_, t_l.at[k]).start()

            @pl.when(jnp.logical_not(self_))
            def _(s_=s_, d_=d_, u=u):
                rc(s_, d_, t_s.at[k, u], t_r.at[k, zj], (base + zc, 2 * c + u)).start()

    def tok_wait(src, dst, k):
        for j in range(2):
            loc = prim & (z == 2 * c + j)

            @pl.when(loc)
            def _(j=j):
                lc(src.at[pl.ds(0, 256)], dst.at[j], t_l.at[k]).wait()

            @pl.when(jnp.logical_not(loc))
            def _(j=j):
                wait_recv(dst.at[j], t_r.at[k, j])
                wait_send(src.at[pl.ds(0, 256)], t_s.at[k, j])

    tok_send(tok, o1, 0)

    def g_start(a, u):
        for r in range(2):
            p1, p2 = pp(r)
            src = g.at[a, u, pl.ds(pl.multiple_of(384 * r + 192 * (1 - p1), 64), 192)]
            rc(src, st1.at[a, u, r], g1_s.at[a, u, r], g1_r.at[a, u, r], nbs(r)[0]).start()

    def quarter(ref, r, q):
        return ref.at[pl.ds(pl.multiple_of(96 * q, 32), 96)]

    def g_step2(a, u):
        for r in range(2):
            p1, p2 = pp(r)
            wait_recv(st1.at[a, u, r], g1_r.at[a, u, r])
            rows = blk(r, p1, 1 - p2)
            part = st1[a, u, r, pl.ds(pl.multiple_of(96 * (1 - p2), 32), 96), :]
            g[a, u, rows, :] = (g[a, u, rows, :].astype(F32) + part.astype(F32)).astype(BF)
            rc(
                g.at[a, u, rows], st2.at[a, u, r], g2_s.at[a, u, r], g2_r.at[a, u, r], nbs(r)[1]
            ).start()

    def g_step3(a, u):
        for r in range(2):
            p1, p2 = pp(r)
            wait_recv(st2.at[a, u, r], g2_r.at[a, u, r])
            rows = blk(r, p1, p2)
            part = st1[a, u, r, pl.ds(pl.multiple_of(96 * p2, 32), 96), :]
            tot = (
                g[a, u, rows, :].astype(F32) + part.astype(F32) + st2[a, u, r].astype(F32)
            ).astype(BF)
            self_ = (c == r) & (z == 2 * c + u)

            @pl.when(self_)
            def _(tot=tot):
                st3[a, z] = tot

            @pl.when(jnp.logical_not(self_))
            def _(tot=tot, rows=rows, r=r):
                g[a, u, rows, :] = tot
                rc(
                    g.at[a, u, rows], st3.at[a, z], g3_s.at[a, u, r], g3_r.at[a, z],
                    (base + r, 2 * c + u),
                ).start()

    q1 = px + c * (py - px)
    q2 = py + c * (px - py)
    e1 = (xn + c * (yn - xn), z)
    e2 = (yn + c * (xn - yn), z)

    def own(r, p1, p2):
        return pl.ds(pl.multiple_of(384 * r + 96 * (2 * p1 + p2), 32), 96)

    def g_step4(a):
        for k in range(4):
            loc = prim & (z == k)

            @pl.when(jnp.logical_not(loc))
            def _(k=k):
                wait_recv(st3.at[a, k], g3_r.at[a, k])

        rb[a] = (
            st3[a, 0].astype(F32)
            + st3[a, 1].astype(F32)
            + st3[a, 2].astype(F32)
            + st3[a, 3].astype(F32)
        ).astype(BF)
        dst = res[a].at[own(c, q1, q2)]
        rc(rb.at[a], dst, ag_s.at[a, 0], ag_r.at[a, 0], e1).start()
        rc(rb.at[a], dst, ag_s.at[a, 1], ag_r.at[a, 1], e2).start()
        rc(rb.at[a], dst, ce_s.at[a, 0], ce_r.at[a, 0], (sib, z)).start()
        lc(rb.at[a], dst, ag_l.at[a]).start()

    def g_step5(a):
        ref = res[a].at[own(c, 1 - q1, q2)]
        wait_recv(ref, ag_r.at[a, 0])
        rc(ref, ref, ag_s.at[a, 2], ag_r.at[a, 2], e2).start()
        rc(ref, ref, ce_s.at[a, 1], ce_r.at[a, 1], (sib, z)).start()

    def g_step6(a):
        ref = res[a].at[own(c, q1, 1 - q2)]
        wait_recv(ref, ag_r.at[a, 1])
        rc(ref, ref, ce_s.at[a, 2], ce_r.at[a, 2], (sib, z)).start()
        ref = res[a].at[own(c, 1 - q1, 1 - q2)]
        wait_recv(ref, ag_r.at[a, 2])
        rc(ref, ref, ce_s.at[a, 3], ce_r.at[a, 3], (sib, z)).start()

    def g_end(a):
        lc(rb.at[a], res[a].at[own(c, q1, q2)], ag_l.at[a]).wait()
        o_ = 1 - c
        for k, rows in enumerate(
            (own(o_, q2, q1), own(o_, 1 - q2, q1), own(o_, q2, 1 - q1), own(o_, 1 - q2, 1 - q1))
        ):
            wait_recv(res[a].at[rows], ce_r.at[a, k])
            wait_send(rb.at[a], ce_s.at[a, k])
        for k in range(3):
            wait_send(rb.at[a], ag_s.at[a, k])
        for u in range(2):
            for r in range(2):
                wait_send(st1.at[a, u, r], g1_s.at[a, u, r])
                wait_send(st2.at[a, u, r], g2_s.at[a, u, r])

                @pl.when(jnp.logical_not((c == r) & (z == 2 * c + u)))
                def _(u=u, r=r):
                    wait_send(st2.at[a, u, r], g3_s.at[a, u, r])

    shared(dl, 1)

    for u in range(2):
        for n in range(3):
            cols = slice(768 * u + 256 * n, 768 * u + 256 * n + 256)
            g[2, u, 256 * n : 256 * n + 256, :] = mm(act[:, cols], dl[...], TN).astype(BF)
        g_start(2, u)

    def dup(t, _):
        u, cols = hidden(t)
        ub = jnp.zeros((1, 256), F32)
        for m in range(2):
            rr = slice(512 * m, 512 * m + 512)
            dv = mm(dl[rr, :], wg[2, u, cols, :], NT) * dg[rr, rows_of(t, 256)].astype(F32)
            dv = dv.astype(BF)
            dg[rr, rows_of(t, 256)] = dv
            ub = ub + jnp.sum(dv.astype(F32), axis=0, keepdims=True)
        vb[0, pl.ds(6 + 2 * c + u, 1), cols] = ub
        return 0

    lax.fori_loop(0, 6, dup, 0)
    partial(
        lambda rows, cols: mm(dg[rows, 0:768], wg[1, 0, cols, :], NT)
        + mm(dg[rows, 768:1536], wg[1, 1, cols, :], NT),
        2,
    )
    for u in range(2):
        for n in range(3):
            g[1, u, 256 * n : 256 * n + 256, :] = mm(
                flow[:, 256 * n : 256 * n + 256], dg[:, 768 * u : 768 * u + 768], TN
            ).astype(BF)
        g_start(1, u)

    wait_send(dl.at[pl.ds(0, 512)], pe_s.at[5])
    def norm1b(m, carry):
        fg, fs, ob = carry
        rr = rows_of(m, 128)
        df = fst[rr, :] + op[rr, :] + rcv[2, rr, :].astype(F32)
        nv = n1[rr, :]
        gg = df * par[1:2, :]
        dr = (
            gg
            - jnp.mean(gg, axis=-1, keepdims=True)
            - nv * jnp.mean(gg * nv, axis=-1, keepdims=True)
        ) * rs1[rr, :]
        fst[rr, :] = dr
        dlo = dr.astype(BF)
        dl[at(mine, m, 128), :] = dlo
        return (
            fg + jnp.sum(df * nv, axis=0, keepdims=True),
            fs + jnp.sum(df, axis=0, keepdims=True),
            ob + jnp.sum(dlo.astype(F32), axis=0, keepdims=True),
        )

    fg, fs, ob = lax.fori_loop(0, 4, norm1b, (ones8, ones8, ones8))
    share(dl, 2)
    vb[0, 3:4, :] = fg
    vb[0, 4:5, :] = fs
    vb[0, 5:6, :] = ob
    shared(dl, 2)
    for u in range(2):
        g_step2(2, u)

    def dmix(m, _):
        rr = rows_of(m, 512)
        dm[rr, :] = mm(dl[rr, :], wo[...], NT).astype(BF)
        return 0

    lax.fori_loop(0, 2, dmix, 0)
    for i in range(3):
        gw = mm(mix[:, 128 * i : 128 * i + 128], dl[...], TN).astype(BF)
        for n, (u, rows) in enumerate((place(2 * i + 1, 3), place(2 * i, 3))):
            g[0, u, rows, :] = gw[64 * n : 64 * n + 64, :]

    def attend_back(i):
        for s in range(2):
            columns(2 * i + s, s)

        def body(t, _):
            rr = rows_of(t, 512)
            uu = []
            for s in range(2):
                w = mm(sort_mat(s, t), dm[:, 128 * i : 128 * i + 128])
                uu.append(
                    (jnp.where(low, 0.0, w) if s == 0 else jnp.where(low, w, 0.0)).astype(BF)
                )
            for s in range(2):
                kv = skv[2 * i + s, rr, :]
                q = sq[2 * i + s, rr, :]
                prob = pr[2 * i + s, rr, :]
                dp = jnp.concatenate(
                    [mm(piece(uu[s], k), piece(kv, k), NT) for k in four], axis=0
                )
                cen = jnp.sum(prob * dp, axis=-1, keepdims=True)
                ds = (prob * (dp - cen)).astype(BF)
                dq = jnp.concatenate([mm(piece(ds, k), piece(kv, k)) for k in four], axis=0) * 0.125
                pb = prob.astype(BF)
                dkv = jnp.concatenate(
                    [
                        mm(
                            jnp.concatenate([piece(pb, k), piece(ds, k)], axis=0),
                            jnp.concatenate([piece(uu[s], k), piece(q, k)], axis=0),
                            TN,
                        )
                        for k in four
                    ],
                    axis=0,
                ).astype(BF)
                if s == 0:
                    ms[s][rr, 0:128] = dkv
                    ms[s][rr, 128:256] = jnp.where(low, dq, 0.0).astype(BF)
                else:
                    ms[s][rr, 0:128] = jnp.where(low, 0.0, dq).astype(BF)
                    ms[s][rr, 128:256] = dkv
            return 0

        lax.fori_loop(0, 2, body, 0)

        def back(t, carry):
            ga = mm(unsort_mat(2 * i, t), ms[0][...])
            gb = mm(unsort_mat(2 * i + 1, t), ms[1][...])
            out = jnp.concatenate(
                [ga[:, 0:128], ga[:, 128:256] + gb[:, 0:128], gb[:, 128:256]], axis=1
            )
            qkv[rows_of(t, 512), 384 * i : 384 * i + 384] = out.astype(BF)
            return carry + jnp.sum(out, axis=0, keepdims=True)

        return lax.fori_loop(0, 2, back, jnp.zeros((1, 384), F32))

    def gqkv(i):
        gw = mm(qkv[:, 384 * i : 384 * i + 384], xall[...], TN).astype(BF)
        for k, (u, rows) in enumerate(pair_rows(i)):
            g[0, u, rows, :] = gw[64 * k : 64 * k + 64, :]

    b0 = attend_back(0)
    gqkv(0)
    for u in range(2):
        g_step3(2, u)
    b1 = attend_back(1)
    gqkv(1)
    g_start(0, 0)
    for u in range(2):
        g_step2(1, u)
    b2 = attend_back(2)
    gqkv(2)
    g_start(0, 1)
    for u in range(2):
        g_step3(1, u)
    g_step4(2)
    bs = (b0, b1, b2)
    rest = jnp.zeros((1, 384), F32)
    for u in range(2):
        heads = range(3 * u, 3 * u + 3)
        qs = [bs[h // 2][:, 128 + 64 * (h % 2) : 192 + 64 * (h % 2)] for h in heads]
        vs = [bs[h // 2][:, 64 + 192 * (h % 2) : 128 + 192 * (h % 2)] for h in heads]
        vb[0, pl.ds(10 + 2 * c + u, 1), :] = jnp.concatenate(qs + vs + [rest], axis=1)

    vdev = (
        (sib, z), (xn, z), (yn, z), (d, z + 1 - 2 * zj), (d, z + 2 - 4 * zc),
    )

    def v_send(k):
        rc(vb.at[k], vr.at[k], v_s.at[k], v_r.at[k], vdev[k]).start()

    def v_add(k):
        wait_recv(vr.at[k], v_r.at[k])
        vb[k + 1] = vb[k] + vr[k]

    v_send(0)
    partial(
        lambda rows, cols: mm(qkv[rows, :], wq[:, cols]),
        3,
    )

    def gin(m, _):
        rr = rows_of(m, 128)
        gtok[rr, :] = (fst[rr, :] + op[rr, :] + rcv[3, rr, :].astype(F32)).astype(BF)
        return 0

    lax.fori_loop(0, 4, gin, 0)
    tok_send(gtok, o2, 1)
    v_add(0)
    v_send(1)
    g_step2(0, 0)
    g_step5(2)
    g_step3(0, 0)
    v_add(1)
    v_send(2)
    g_step2(0, 1)
    g_step6(2)
    g_step4(1)
    v_add(2)
    v_send(3)
    g_step3(0, 1)
    g_step5(1)
    v_add(3)
    v_send(4)
    g_step6(1)
    g_step4(0)
    g_step5(0)
    v_add(4)
    vout[...] = vb[5]
    vout[14:15, :] = vb[5, pl.ds(6 + z, 1), :]
    vout[15:16, :] = vb[5, pl.ds(10 + z, 1), :]
    g_step6(0)
    for a in range(3):
        g_end(a)
    tok_wait(tok, o1, 0)
    tok_wait(gtok, o2, 1)

    for a in range(1, 3):
        w_end(a)
    for k in range(4):
        wait_send(xrows(k, c), cx_s.at[k])
        if k >= 2:
            wait_send(rcv.at[k], pe_s.at[k])
    for k in (0, 2):
        wait_send(flow.at[pl.ds(0, 512)], pe_s.at[4 + k])
    for k in range(5):
        wait_send(vb.at[k], v_s.at[k])
    for j in range(2):

        @pl.when(jnp.logical_not(prim & (z == 2 * c + j)))
        def _(j=j):
            wait_send(ord_in, o_s.at[j])

    @pl.when(prim)
    def _():
        for k in range(3):
            wait_send(bias_in, b_s.at[k])
        wait_send(mr_in, m_s.at[0])
        wait_send(mg_in, m_s.at[1])


def layer(x, order, wqkv, wout, wb, wc, mr, mg, *small):
    dma = pltpu.SemaphoreType.DMA
    hbm = pl.BlockSpec(memory_space=pl.ANY)
    vmem = pl.BlockSpec(memory_space=pltpu.VMEM)
    V = pltpu.VMEM
    return pl.pallas_call(
        kernel,
        out_shape=(
            jax.ShapeDtypeStruct((2, 256, 768), BF),
            jax.ShapeDtypeStruct((2, 256, 768), BF),
            jax.ShapeDtypeStruct((768, 768), BF),
            jax.ShapeDtypeStruct((768, 768), BF),
            jax.ShapeDtypeStruct((768, 768), BF),
            jax.ShapeDtypeStruct((16, 768), F32),
        ),
        in_specs=[hbm] * 8 + [vmem] * 8,
        out_specs=(hbm, hbm, hbm, hbm, hbm, vmem),
        scratch_shapes=[
            V((1024, 768), BF),
            V((256, 2, 768), BF),
            V((2, 3, 2, 1024), jnp.int32),
            V((3, 2, 768, 768), BF),
            V((2, 8, 768), F32),
            V((8, 768), F32),
            V((8, 768), F32),
            V(mr.shape, jnp.int32),
            V(mg.shape, BF),
            V((mg.shape[0], 768), BF),
            V((1152, 768), BF),
            V((384, 768), BF),
            V((1024, 1152), BF),
            V((2, 1024, 128), jnp.int32),
            V((6, 1024, 128), BF),
            V((6, 1024, 128), BF),
            V((6, 1024, 128), F32),
            V((1024, 384), BF),
            V((2, 512, 768), BF),
            V((4, 512, 768), BF),
            V((512, 768), F32),
            V((512, 768), F32),
            V((512, 768), F32),
            V((512, 1), F32),
            V((1024, 768), BF),
            V((1024, 1536), BF),
            V((1024, 1536), BF),
            V((1024, 768), BF),
            V((3, 2, 768, 768), BF),
            V((3, 2, 2, 192, 768), BF),
            V((3, 2, 2, 96, 768), BF),
            V((3, 4, 96, 768), BF),
            V((3, 96, 768), BF),
            V((6, 16, 768), F32),
            V((5, 16, 768), F32),
            dma((2, 2)), dma((4,)), dma, dma((4,)), dma((4,)),
            dma((2,)), dma((2,)), dma,
            dma((3,)), dma((2,)), dma,
            dma((2,)), dma((2,)), dma((2,)),
            dma((3, 2, 2)), dma((3, 2, 2)), dma((3, 2, 2)),
            dma((3, 2, 2, 3)), dma((3, 2, 2, 3)), dma((4,)),
            dma((7,)), dma((7,)),
            dma((2, 2)), dma((2, 2)), dma((2,)),
            dma((5,)), dma((5,)),
            dma((3, 2, 2)), dma((3, 2, 2)), dma((3, 2, 2)), dma((3, 2, 2)),
            dma((3, 2, 2)), dma((3, 4)), dma((3, 3)), dma((3, 3)), dma((3,)),
            dma((3, 4)), dma((3, 4)),
        ],
        compiler_params=pltpu.CompilerParams(
            collective_id=0, has_side_effects=True, vmem_limit_bytes=60 * 2**20
        ),
    )(x, order, wqkv, wout, wb, wc, mr, mg, *small)


def finish_kernel(
    o1, o2, ra, rb, rc, vec, out, gin, gq, go, gb, gc, fg, fs, ob, db, sg, ss, ub, qv,
    o1v, o2v, rv, outv, ginv, gv, in_sem, out_sem,
):
    loads = [
        pltpu.make_async_copy(a, b, in_sem.at[k])
        for k, (a, b) in enumerate(
            ((o1, o1v), (o2, o2v), (ra, rv.at[0]), (rb, rv.at[1]), (rc, rv.at[2]))
        )
    ]
    for k in (2, 3, 4, 1, 0):
        loads[k].start()
    stores = [
        pltpu.make_async_copy(a, b, out_sem.at[k])
        for k, (a, b) in enumerate(
            (
                (gv.at[0, pl.ds(0, 576)], gq), (gv.at[0, pl.ds(576, 192)], go),
                (gv.at[1], gb), (gv.at[2], gc), (ginv, gin), (outv, out),
            )
        )
    ]
    for ref, row in ((sg, 0), (ss, 1), (db, 2), (fg, 3), (fs, 4), (ob, 5), (ub, 14)):
        ref[...] = vec[row, :]
    wide = qv.shape[1]
    qv[0:1, :] = vec[15:16, 0:wide]
    qv[1:2, :] = vec[15:16, wide : 2 * wide]

    for a in range(3):
        loads[2 + a].wait()

        def body(k, _, a=a):
            rr = pl.ds(pl.multiple_of(k * 96, 96), 96)
            gv[a, rr, :] = rv[a, rr, :].astype(F32)
            return 0

        lax.fori_loop(0, 8, body, 0)
        if a == 0:
            stores[0].start()
            stores[1].start()
        else:
            stores[a + 1].start()

    def weave(src, dst, dtype):
        def body(k, _):
            rr = pl.ds(pl.multiple_of(k * 32, 32), 32)
            both = jnp.stack([src[0, rr, :].astype(F32), src[1, rr, :].astype(F32)], axis=1)
            dst[rr] = both.astype(dtype)
            return 0

        lax.fori_loop(0, 8, body, 0)

    loads[1].wait()
    weave(o2v, ginv, F32)
    stores[4].start()
    loads[0].wait()
    weave(o1v, outv, BF)
    stores[5].start()
    for cp in stores:
        cp.wait()


def finish(o1, o2, ra, rb, rc, vec):
    hbm = pl.BlockSpec(memory_space=pl.ANY)
    vmem = pl.BlockSpec(memory_space=pltpu.VMEM)
    V = pltpu.VMEM
    S = jax.ShapeDtypeStruct
    row = S((768,), F32)
    return pl.pallas_call(
        finish_kernel,
        out_shape=(
            S((256, 2, 768), BF), S((256, 2, 768), F32), S((576, 768), F32), S((192, 768), F32),
            S((768, 768), F32), S((768, 768), F32), row, row, row, row, row, row, row,
            S((2, 192), F32),
        ),
        in_specs=[hbm] * 5 + [vmem],
        out_specs=(hbm,) * 6 + (vmem,) * 8,
        scratch_shapes=[
            V((2, 256, 768), BF), V((2, 256, 768), BF), V((3, 768, 768), BF),
            V((256, 2, 768), BF), V((256, 2, 768), F32), V((3, 768, 768), F32),
            pltpu.SemaphoreType.DMA((5,)), pltpu.SemaphoreType.DMA((6,)),
        ],
        compiler_params=pltpu.CompilerParams(vmem_limit_bytes=60 * 2**20),
    )(o1, o2, ra, rb, rc, vec)


def shards(
    inputs, qkv_weight, qv_bias, out_weight, out_bias, first_gain, first_shift,
    first_layer_weight, first_layer_bias, second_layer_weight, second_layer_bias,
    second_gain, second_shift, cluster_order, masked_rows, masked_grad,
):
    t = lax.axis_index("tensor")
    heads = qkv_weight.shape[2]
    wqkv = qkv_weight.transpose(1, 2, 0).reshape(3 * heads, 768)
    order = cluster_order.transpose(1, 0, 2)

    o1, o2, ra, rb, rc, vec = layer(
        inputs, order, wqkv, out_weight, first_layer_weight, second_layer_weight,
        masked_rows, masked_grad.transpose(1, 0, 2), qv_bias,
        out_bias, first_gain, first_shift, second_layer_bias, second_gain, second_shift,
        first_layer_bias,
    )

    many = lax.axis_size("dp") // 8
    if many > 1:
        groups = [[8 * i + j for i in range(many)] for j in range(8)]
        ra, rb, rc = lax.psum(
            (ra.astype(F32), rb.astype(F32), rc.astype(F32)), "dp", axis_index_groups=groups
        )
        ra, rb, rc = ra.astype(BF), rb.astype(BF), rc.astype(BF)
        vec = lax.psum(vec, "dp", axis_index_groups=groups)
    outputs, grad_inputs, gq, go, gb, gc, fg, fs, ob, db, sg, ss, ub, qv = finish(
        o1, o2, ra, rb, rc, vec
    )
    return (
        outputs,
        grad_inputs,
        gq.reshape(3, heads, 768).transpose(2, 0, 1),
        qv,
        go,
        ob,
        fg,
        fs,
        gb,
        ub,
        gc,
        db,
        sg,
        ss,
    )


def solution(mesh):
    placed = (
        P("tensor", "dp", None), P(None, None, "tensor"), P(None, "tensor"), P("tensor", None),
        P(), P(), P(), P(None, "tensor"), P("tensor"), P("tensor", None), P(), P(), P(),
        P("dp", "tensor", None), P("dp", None), P("dp", None, None),
    )
    return jax.shard_map(
        shards,
        mesh=mesh,
        in_specs=placed,
        out_specs=(
            P("tensor", "dp", None), P("tensor", "dp", None), P(None, None, "tensor"),
            P(None, "tensor"), P("tensor", None), P(), P(), P(), P(None, "tensor"), P("tensor"),
            P("tensor", None), P(), P(), P(),
        ),
        check_vma=False,
    )
```

```python
import math

import jax
import jax.numpy as jnp
from jax import lax
from jax.experimental import pallas as pl
from jax.experimental.pallas import tpu as pltpu
from jax.sharding import PartitionSpec as P

HD = 64
C = 128
NORM_EPS = 1e-05
BF = jnp.bfloat16
F32 = jnp.float32
MESH = pl.DeviceIdType.MESH
DIRECT = (2,)
RSQRT2 = 1.0 / math.sqrt(2.0)
RSQRT2PI = 1.0 / math.sqrt(2.0 * math.pi)

NN = (((1,), (0,)), ((), ()))
NT = (((1,), (1,)), ((), ()))
TN = (((0,), (0,)), ((), ()))


def mm(a, b, dims=NN):
    return lax.dot_general(a, b, dims, preferred_element_type=F32)


def kernel(
    x_in, ord_in, wq_in, wo_in, wb_in, wc_in, mr_in, mg_in, qb_in,
    p0, p1_, p2_, p3_, p4_, p5_, p6_,
    o1, o2, ra, rbb, rcc, vout,
    xall, x3, ordv, wg, bias, bias_in, par, mr, mg3, mg, wq, wo, qkv, oc, sq, skv, pr, mix,
    snd, rcv, op, fst, n1, rs1, flow, act, dg, dl, g, st1, st2, st3,
    rb, vb, vr,
    x_s, x_r, x_l, cx_s, cx_r, o_s, o_r, o_l, b_s, b_r, b_l, m_s, m_r, m_l,
    wz_s, wz_s2, wz_s3, wz_r, wx_s, wx_r, w_l, pe_s, pe_r, t_s, t_r, t_l, v_s, v_r,
    g1_s, g1_r, g2_s, g2_r, g3_s, g3_r, ag_s, ag_r, ag_l, ce_s, ce_r,
):
    w_in = (None, wb_in, wc_in)
    res = (ra, rbb, rcc)
    dm = act.at[:, 0:384]
    ms = (act.at[:, 512:768], act.at[:, 768:1024])
    tok = wg.at[0, 0, pl.ds(0, 512)]
    gtok = wg.at[0, 1, pl.ds(0, 512)]
    d = lax.axis_index("dp")
    z = lax.axis_index("tensor")
    c = lax.rem(d, 2)
    base = d - c
    sib = base + 1 - c
    px = lax.rem(lax.div(d, 2), 2)
    py = lax.rem(lax.div(d, 4), 2)
    xn = d + 2 - 4 * px
    yn = d + 4 - 8 * py
    zc = lax.div(z, 2)
    zj = lax.rem(z, 2)
    up = 1 - 2 * c
    zz = 3 * c + z * up
    prim = zc == c

    def rc(src, dst, ss, rs, dev):
        return pltpu.make_async_remote_copy(
            src_ref=src, dst_ref=dst, send_sem=ss, recv_sem=rs,
            device_id=dev, device_id_type=MESH,
        )

    def wait_send(src, ss):
        rc(src, src, ss, ss, (sib, z)).wait_send()

    def wait_recv(dst, rs):
        rc(dst, dst, rs, rs, (sib, z)).wait_recv()

    def lc(src, dst, sem):
        return pltpu.make_async_copy(src, dst, sem)

    bar = pltpu.get_barrier_semaphore()
    for k in range(1, 8):
        oc_, oz = k % 2, k // 2
        dev = (base + lax.rem(c + oc_, 2), lax.rem(z + oz, 4))
        pl.semaphore_signal(bar, inc=1, device_id=dev, device_id_type=MESH)
    for dev in ((xn, z), (yn, z)):
        pl.semaphore_signal(bar, inc=1, device_id=dev, device_id_type=MESH)
    pl.semaphore_wait(bar, 9)

    def pp(r):
        return (px, py) if r == 0 else (py, px)

    def nbs(r):
        return ((xn, z), (yn, z)) if r == 0 else ((yn, z), (xn, z))

    def blk(r, p1, p2):
        return pl.ds(pl.multiple_of(384 * r + 96 * (2 * p1 + p2), 32), 96)

    def uof(v):
        return c + v * up

    def w_start(a):
        for v in range(2):
            for r in range(2):
                p1, p2 = pp(r)
                rows = blk(r, p1, p2)
                dst = wg.at[a, uof(v), rows]
                if a > 0:
                    parts = ((zz == v, w_in[a].at[rows]),)
                elif r == 0:
                    parts = ((zz == v, wq_in.at[rows]),)
                else:
                    off = pl.ds(pl.multiple_of(96 * p2, 32), 96)
                    high = pl.ds(pl.multiple_of(384 + 96 * p2, 32), 96)
                    parts = (
                        ((zz == v) & (p1 == 0), wq_in.at[high]),
                        ((zz == v) & (p1 == 1), wo_in.at[off]),
                    )
                near = z + up if v == 0 else z - up
                far = z + 2 * up if v == 0 else z + up
                last = z + (3 - v) * up
                for cond, src in parts:

                    @pl.when(cond)
                    def _(src=src, dst=dst, v=v, r=r, near=near, far=far, last=last):
                        rc(src, dst, wz_s.at[a, v, r], wz_r.at[a, v, r], (d, near)).start()
                        rc(src, dst, wz_s2.at[a, v, r], wz_r.at[a, v, r], (d, far)).start()
                        if a in DIRECT:
                            rc(src, dst, wz_s3.at[v, r], wz_r.at[a, v, r], (d, last)).start()

    def w_copies(a, v):
        if a > 0:
            return (lc(w_in[a], wg.at[a, uof(v)], w_l.at[a]),)
        return (
            lc(wq_in, wg.at[0, uof(v), pl.ds(0, 576)], w_l.at[0]),
            lc(wo_in, wg.at[0, uof(v), pl.ds(576, 192)], w_l.at[3]),
        )

    def w_local(a):
        for v in range(2):

            @pl.when(zz == v)
            def _(v=v):
                for cp in w_copies(a, v):
                    cp.start()

    def w_fwd(a, stage):
        for v in range(2):
            for r in range(2):
                p1, p2 = pp(r)
                ref = wg.at[a, uof(v), blk(r, p1, p2)]
                n1_, n2_ = nbs(r)
                cond = (zz == 3) if stage else ((zz == 1 - v) | (zz == 2))
                if a in DIRECT:
                    cond = zz != v

                @pl.when(cond)
                def _(ref=ref, v=v, r=r, n1_=n1_, n2_=n2_):
                    wait_recv(ref, wz_r.at[a, v, r])
                    rc(ref, ref, wx_s.at[a, v, r, 0], wx_r.at[a, v, r, 0], n1_).start()
                    rc(ref, ref, wx_s.at[a, v, r, 1], wx_r.at[a, v, r, 1], n2_).start()

                if not stage and a not in DIRECT:

                    @pl.when(zz == 2)
                    def _(ref=ref, v=v, r=r):
                        rc(ref, ref, wz_s.at[a, v, r], wz_r.at[a, v, r], (d, z + up)).start()

    def w_fwd2(a):
        for v in range(2):
            for r in range(2):
                p1, p2 = pp(r)
                ref = wg.at[a, uof(v), blk(r, 1 - p1, p2)]
                n1_, n2_ = nbs(r)

                @pl.when(zz != v)
                def _(ref=ref, v=v, r=r, n2_=n2_):
                    wait_recv(ref, wx_r.at[a, v, r, 0])
                    rc(ref, ref, wx_s.at[a, v, r, 2], wx_r.at[a, v, r, 2], n2_).start()

    def w_done(a):
        for v in range(2):
            for r in range(2):
                p1, p2 = pp(r)

                @pl.when(zz != v)
                def _(v=v, r=r, p1=p1, p2=p2):
                    wait_recv(wg.at[a, uof(v), blk(r, p1, 1 - p2)], wx_r.at[a, v, r, 1])
                    wait_recv(wg.at[a, uof(v), blk(r, 1 - p1, 1 - p2)], wx_r.at[a, v, r, 2])

            @pl.when(zz == v)
            def _(v=v):
                for cp in w_copies(a, v):
                    cp.wait()

    def w_end(a):
        for v in range(2):
            for r in range(2):
                p1, p2 = pp(r)
                ref = wg.at[a, uof(v), blk(r, p1, p2)]

                @pl.when((zz == v) if a in DIRECT else ((zz == v) | (zz == 2)))
                def _(ref=ref, v=v, r=r):
                    wait_send(ref, wz_s.at[a, v, r])

                @pl.when(zz == v)
                def _(ref=ref, v=v, r=r):
                    wait_send(ref, wz_s2.at[a, v, r])
                    if a in DIRECT:
                        wait_send(ref, wz_s3.at[v, r])

                @pl.when(zz != v)
                def _(ref=ref, v=v, r=r):
                    for k in range(3):
                        wait_send(ref, wx_s.at[a, v, r, k])

    w_start(0)
    w_local(0)
    lc(x_in, x3, x_l).start()
    for k, ref in enumerate((p0, p1_, p2_, p3_, p4_, p5_)):
        par[k : k + 1, :] = ref[...].astype(F32).reshape(1, 768)
    bias_in[...] = jnp.zeros((8, 768), F32)
    bias_in[0:2, 0:192] = qb_in[...].astype(F32)
    bias_in[2:3, :] = p6_[...].astype(F32).reshape(1, 768)

    for j in range(2):
        dev = (base + zc, 2 * c + j)
        self_ = (zc == c) & (z == 2 * c + j)

        @pl.when(self_)
        def _(j=j):
            lc(ord_in, ordv.at[zj], o_l).start()

        @pl.when(jnp.logical_not(self_))
        def _(j=j, dev=dev):
            rc(ord_in, ordv.at[lax.rem(z, 2)], o_s.at[j], o_r.at[zj], dev).start()

    @pl.when(prim)
    def _():
        for k in range(1, 4):
            dev = (d, lax.rem(z + k, 4))
            rc(bias_in, bias.at[zj], b_s.at[k - 1], b_r.at[zj], dev).start()
        lc(bias_in, bias.at[zj], b_l).start()
        lc(mr_in, mr, m_l.at[0]).start()
        lc(mg_in, mg3, m_l.at[1]).start()
        rc(mr_in, mr, m_s.at[0], m_r.at[0], (sib, z)).start()
        rc(mg_in, mg3, m_s.at[1], m_r.at[1], (sib, z)).start()


    w_local(1)
    w_local(2)
    lc(x_in, x3, x_l).wait()

    def part(k, _):
        both = x3[pl.ds(pl.multiple_of(32 * k, 32), 32)].astype(F32)
        for j in range(2):
            dg[pl.ds(pl.multiple_of(256 * j + 32 * k, 32), 32), 0:768] = both[:, j, :].astype(BF)
        return 0

    lax.fori_loop(0, 8, part, 0)
    for j in range(2):
        for h in range(2):
            zt = 2 * c + j
            rows = pl.ds(128 * h, 128)
            self_ = (c == h) & (z == zt)
            src = dg.at[pl.ds(256 * j + 128 * h, 128), 0:768]
            dst = xall.at[pl.ds(pl.multiple_of(256 * z + 128 * h, 128), 128)]

            @pl.when(self_)
            def _(src=src, dst=dst):
                lc(src, dst, x_l).start()

            @pl.when(jnp.logical_not(self_))
            def _(src=src, dst=dst, j=j, h=h, zt=zt):
                rc(src, dst, x_s.at[j, h], x_r.at[z], (base + h, zt)).start()

    w_fwd(0, 0)
    w_fwd(0, 1)
    w_fwd2(0)

    def xrows(k, h):
        return xall.at[pl.ds(pl.multiple_of(256 * k + 128 * h, 128), 128)]

    for k in range(4):
        ref = xrows(k, c)
        loc = prim & (z == k)

        @pl.when(loc)
        def _(ref=ref):
            lc(ref, ref, x_l).wait()

        @pl.when(jnp.logical_not(loc))
        def _(ref=ref, k=k):
            wait_recv(ref, x_r.at[k])

        rc(ref, ref, cx_s.at[k], cx_r.at[k], (sib, z)).start()
    w_start(1)
    for k in range(4):
        wait_recv(xrows(k, 1 - c), cx_r.at[k])

    for u in range(2):
        loc = prim & (zj == u)

        @pl.when(loc)
        def _(u=u):
            lc(ord_in, ordv.at[u], o_l).wait()
            lc(bias_in, bias.at[u], b_l).wait()

        @pl.when(jnp.logical_not(loc))
        def _(u=u):
            wait_recv(ordv.at[u], o_r.at[u])
            wait_recv(bias.at[u], b_r.at[u])

    @pl.when(prim)
    def _():
        lc(mr_in, mr, m_l.at[0]).wait()
        lc(mg_in, mg3, m_l.at[1]).wait()

    @pl.when(jnp.logical_not(prim))
    def _():
        wait_recv(mr, m_r.at[0])
        wait_recv(mg3, m_r.at[1])

    both = mg3[...].astype(F32)
    mg[...] = jnp.where(zj == 0, both[:, 0, :], both[:, 1, :]).astype(BF)
    w_done(0)

    lane = lax.broadcasted_iota(jnp.int32, (512, 128), 1)
    sub = lax.broadcasted_iota(jnp.int32, (512, 1024), 0)
    low = lane < 64

    def place(h, kind):
        return h // 3, slice(192 * kind + 64 * (h % 3), 192 * kind + 64 * (h % 3) + 64)

    def pair_rows(i):
        a, b = 2 * i, 2 * i + 1
        return (place(a, 1), place(a, 2), place(a, 0), place(b, 0), place(b, 2), place(b, 1))

    for i in range(3):
        for n, (u, rows) in enumerate(pair_rows(i)):
            wq[384 * i + 64 * n : 384 * i + 64 * n + 64, :] = wg[0, u, rows, :]
        for n, (u, rows) in enumerate((place(2 * i + 1, 3), place(2 * i, 3))):
            wo[128 * i + 64 * n : 128 * i + 64 * n + 64, :] = wg[0, u, rows, :]

    def bq(i):
        nil = jnp.zeros((1, 64), F32)

        def take(h, row):
            return bias[h // 3, row : row + 1, 64 * (h % 3) : 64 * (h % 3) + 64]

        a, b = 2 * i, 2 * i + 1
        return jnp.concatenate(
            [nil, take(a, 1), take(a, 0), take(b, 0), take(b, 1), nil], axis=1
        )

    def rows_of(m, n):
        return pl.ds(pl.multiple_of(m * n, n), n)

    for lo_, hi_ in ((0, 2), (2, 3)):
        bv = jnp.concatenate([bq(i) for i in range(lo_, hi_)], axis=1)
        cols = slice(384 * lo_, 384 * hi_)

        def body(k, _, cols=cols, bv=bv):
            rr = rows_of(k, 512)
            qkv[rr, cols] = (mm(xall[rr, :], wq[cols, :], NT) + bv).astype(BF)
            return 0

        lax.fori_loop(0, 2, body, 0)

    w_fwd(1, 0)
    w_start(2)

    def columns(h, s):
        row = ordv[h // 3, h % 3, pl.ds(zj, 1), :]
        oc[s] = jnp.broadcast_to(row, (128, 1024)).T

    def sort_mat(s, t):
        b = oc[s, rows_of(t, 512), :]
        return jnp.concatenate(
            [jnp.where(b == lane + 128 * k, 1.0, 0.0).astype(BF) for k in range(8)], axis=1
        )

    def unsort_mat(h, t):
        row = ordv[h // 3, h % 3, pl.ds(zj, 1), :]
        return jnp.where(sub + 512 * t == row, 1.0, 0.0).astype(BF)

    four = range(4)

    def piece(w, k):
        return w[128 * k : 128 * k + 128]

    def attend(i):
        for s in range(2):
            columns(2 * i + s, s)

        def body(t, _):
            rr = rows_of(t, 512)
            q, kv = [], []
            for s in range(2):
                at_ = 384 * i + 128 * s
                w = mm(sort_mat(s, t), qkv[:, at_ : at_ + 256])
                if s == 0:
                    kv.append(w[:, 0:128].astype(BF))
                    q.append((jnp.where(low, w[:, 128:256], 0.0) * 0.125).astype(BF))
                else:
                    q.append((jnp.where(low, 0.0, w[:, 0:128]) * 0.125).astype(BF))
                    kv.append(w[:, 128:256].astype(BF))
                sq[2 * i + s, rr, :] = q[s]
                skv[2 * i + s, rr, :] = kv[s]
            for s in range(2):
                sc = [mm(piece(q[s], k), piece(kv[s], k), NT) for k in four]
                sc = jnp.concatenate(sc, axis=0)
                ex = jnp.exp(sc - jnp.max(sc, axis=-1, keepdims=True))
                prob = ex * (1.0 / jnp.sum(ex, axis=-1, keepdims=True))
                pr[2 * i + s, rr, :] = prob
                pb = prob.astype(BF)
                mx = jnp.concatenate([mm(piece(pb, k), piece(kv[s], k)) for k in four], axis=0)
                keep = jnp.where(low, 0.0, mx) if s == 0 else jnp.where(low, mx, 0.0)
                ms[s][rr, 0:128] = keep.astype(BF)
            return 0

        lax.fori_loop(0, 2, body, 0)

        def back(t, _):
            both = mm(unsort_mat(2 * i, t), ms[0][:, 0:128]) + mm(
                unsort_mat(2 * i + 1, t), ms[1][:, 0:128]
            )
            mix[rows_of(t, 512), 128 * i : 128 * i + 128] = both.astype(BF)
            return 0

        lax.fori_loop(0, 2, back, 0)

    attend(0)
    w_fwd(1, 1)
    attend(1)
    w_fwd2(1)
    w_fwd(2, 0)
    attend(2)

    mine = 512 * c
    other = 512 - mine

    def at(off, m, n):
        return pl.ds(pl.multiple_of(off + m * n, n), n)

    def partial(fn, k):
        if k >= 2:
            wait_send(snd.at[k % 2], pe_s.at[k - 2])
        for n in range(3):
            cols = slice(256 * n, 256 * n + 256)
            snd[k % 2, :, cols] = fn(at(other, 0, 512), cols).astype(BF)
        rc(snd.at[k % 2], rcv.at[k], pe_s.at[k], pe_r.at[k], (sib, z)).start()
        for n in range(3):
            cols = slice(256 * n, 256 * n + 256)
            op[:, cols] = fn(at(mine, 0, 512), cols)
        wait_recv(rcv.at[k], pe_r.at[k])

    def share(ref, k):
        own = ref.at[pl.ds(pl.multiple_of(mine, 512), 512)]
        rc(own, own, pe_s.at[4 + k], pe_r.at[4 + k], (sib, z)).start()

    def shared(ref, k):
        wait_recv(ref.at[pl.ds(pl.multiple_of(other, 512), 512)], pe_r.at[4 + k])

    partial(lambda rows, cols: mm(mix[rows, :], wo[:, cols]), 0)

    def norm1(m, _):
        rr = rows_of(m, 128)
        v = (
            xall[at(mine, m, 128), :].astype(F32)
            + op[rr, :]
            + rcv[0, rr, :].astype(F32)
            + par[0:1, :]
        )
        cen = v - jnp.mean(v, axis=-1, keepdims=True)
        rstd = lax.rsqrt(jnp.mean(cen * cen, axis=-1, keepdims=True) + NORM_EPS)
        nv = cen * rstd
        n1[rr, :] = nv
        rs1[rr, :] = rstd
        fv = nv * par[1:2, :] + par[2:3, :]
        fst[rr, :] = fv
        flow[at(mine, m, 128), :] = fv.astype(BF)
        return 0

    lax.fori_loop(0, 4, norm1, 0)
    share(flow, 0)
    w_done(1)

    for j in range(2):
        for h in range(2):

            @pl.when(jnp.logical_not((c == h) & (z == 2 * c + j)))
            def _(j=j, h=h):
                wait_send(dg.at[pl.ds(0, 128), 0:768], x_s.at[j, h])

    def hidden(t):
        return lax.div(t, 3), rows_of(lax.rem(t, 3), 256)

    def ffn_up(off):
        def body(t, _):
            u, cols = hidden(t)
            rr = at(off, 0, 512)
            h = mm(flow[rr, :], wg[1, u, :, cols]) + bias[u, 2:3, cols]
            cdf = 0.5 + 0.5 * lax.erf(h * RSQRT2)
            act[rr, rows_of(t, 256)] = (h * cdf).astype(BF)
            dg[rr, rows_of(t, 256)] = (cdf + h * (jnp.exp(-0.5 * h * h) * RSQRT2PI)).astype(BF)
            return 0

        lax.fori_loop(0, 6, body, 0)

    ffn_up(mine)
    w_fwd2(2)
    shared(flow, 0)
    ffn_up(other)
    w_done(2)
    partial(
        lambda rows, cols: mm(act[rows, 0:768], wg[2, 0, :, cols])
        + mm(act[rows, 768:1536], wg[2, 1, :, cols]),
        1,
    )

    w_end(0)

    vb[0] = jnp.zeros((16, 768), F32)
    ones8 = jnp.zeros((1, 768), F32)

    def norm2(m, carry):
        sgain, sshift, dbias = carry
        rr = rows_of(m, 128)
        v = fst[rr, :] + op[rr, :] + rcv[1, rr, :].astype(F32) + par[3:4, :]
        cen = v - jnp.mean(v, axis=-1, keepdims=True)
        rstd = lax.rsqrt(jnp.mean(cen * cen, axis=-1, keepdims=True) + NORM_EPS)
        nv = cen * rstd
        tok[rr, :] = (nv * par[4:5, :] + par[5:6, :]).astype(BF)
        pos = lax.broadcasted_iota(jnp.int32, (128, mr.shape[1]), 0) + (mine + 128 * m)
        hits = jnp.where(pos == mr[pl.ds(zj, 1), :], 1.0, 0.0).astype(BF)
        dout = mm(hits, mg[...])
        gg = dout * par[4:5, :]
        d2 = (
            gg
            - jnp.mean(gg, axis=-1, keepdims=True)
            - nv * jnp.mean(gg * nv, axis=-1, keepdims=True)
        ) * rstd
        fst[rr, :] = d2
        dlo = d2.astype(BF)
        dl[at(mine, m, 128), :] = dlo
        return (
            sgain + jnp.sum(dout * nv, axis=0, keepdims=True),
            sshift + jnp.sum(dout, axis=0, keepdims=True),
            dbias + jnp.sum(dlo.astype(F32), axis=0, keepdims=True),
        )

    sg, ss, db = lax.fori_loop(0, 4, norm2, (ones8, ones8, ones8))
    share(dl, 1)
    vb[0, 0:1, :] = sg
    vb[0, 1:2, :] = ss
    vb[0, 2:3, :] = db

    def tok_send(src, dst, k):
        for u in range(2):
            self_ = prim & (z == 2 * c + u)
            s_ = src.at[pl.ds(256 * u, 256)]
            d_ = dst.at[zj]

            @pl.when(self_)
            def _(s_=s_, d_=d_):
                lc(s_, d_, t_l.at[k]).start()

            @pl.when(jnp.logical_not(self_))
            def _(s_=s_, d_=d_, u=u):
                rc(s_, d_, t_s.at[k, u], t_r.at[k, zj], (base + zc, 2 * c + u)).start()

    def tok_wait(src, dst, k):
        for j in range(2):
            loc = prim & (z == 2 * c + j)

            @pl.when(loc)
            def _(j=j):
                lc(src.at[pl.ds(0, 256)], dst.at[j], t_l.at[k]).wait()

            @pl.when(jnp.logical_not(loc))
            def _(j=j):
                wait_recv(dst.at[j], t_r.at[k, j])
                wait_send(src.at[pl.ds(0, 256)], t_s.at[k, j])

    tok_send(tok, o1, 0)

    def g_start(a, u):
        for r in range(2):
            p1, p2 = pp(r)
            src = g.at[a, u, pl.ds(pl.multiple_of(384 * r + 192 * (1 - p1), 64), 192)]
            rc(src, st1.at[a, u, r], g1_s.at[a, u, r], g1_r.at[a, u, r], nbs(r)[0]).start()

    def quarter(ref, r, q):
        return ref.at[pl.ds(pl.multiple_of(96 * q, 32), 96)]

    def g_step2(a, u):
        for r in range(2):
            p1, p2 = pp(r)
            wait_recv(st1.at[a, u, r], g1_r.at[a, u, r])
            rows = blk(r, p1, 1 - p2)
            part = st1[a, u, r, pl.ds(pl.multiple_of(96 * (1 - p2), 32), 96), :]
            g[a, u, rows, :] = (g[a, u, rows, :].astype(F32) + part.astype(F32)).astype(BF)
            rc(
                g.at[a, u, rows], st2.at[a, u, r], g2_s.at[a, u, r], g2_r.at[a, u, r], nbs(r)[1]
            ).start()

    def g_step3(a, u):
        for r in range(2):
            p1, p2 = pp(r)
            wait_recv(st2.at[a, u, r], g2_r.at[a, u, r])
            rows = blk(r, p1, p2)
            part = st1[a, u, r, pl.ds(pl.multiple_of(96 * p2, 32), 96), :]
            tot = (
                g[a, u, rows, :].astype(F32) + part.astype(F32) + st2[a, u, r].astype(F32)
            ).astype(BF)
            self_ = (c == r) & (z == 2 * c + u)

            @pl.when(self_)
            def _(tot=tot):
                st3[a, z] = tot

            @pl.when(jnp.logical_not(self_))
            def _(tot=tot, rows=rows, r=r):
                g[a, u, rows, :] = tot
                rc(
                    g.at[a, u, rows], st3.at[a, z], g3_s.at[a, u, r], g3_r.at[a, z],
                    (base + r, 2 * c + u),
                ).start()

    q1 = px + c * (py - px)
    q2 = py + c * (px - py)
    e1 = (xn + c * (yn - xn), z)
    e2 = (yn + c * (xn - yn), z)

    def own(r, p1, p2):
        return pl.ds(pl.multiple_of(384 * r + 96 * (2 * p1 + p2), 32), 96)

    def g_step4(a):
        for k in range(4):
            loc = prim & (z == k)

            @pl.when(jnp.logical_not(loc))
            def _(k=k):
                wait_recv(st3.at[a, k], g3_r.at[a, k])

        rb[a] = (
            st3[a, 0].astype(F32)
            + st3[a, 1].astype(F32)
            + st3[a, 2].astype(F32)
            + st3[a, 3].astype(F32)
        ).astype(BF)
        dst = res[a].at[own(c, q1, q2)]
        rc(rb.at[a], dst, ag_s.at[a, 0], ag_r.at[a, 0], e1).start()
        rc(rb.at[a], dst, ag_s.at[a, 1], ag_r.at[a, 1], e2).start()
        rc(rb.at[a], dst, ce_s.at[a, 0], ce_r.at[a, 0], (sib, z)).start()
        lc(rb.at[a], dst, ag_l.at[a]).start()

    def g_step5(a):
        ref = res[a].at[own(c, 1 - q1, q2)]
        wait_recv(ref, ag_r.at[a, 0])
        rc(ref, ref, ag_s.at[a, 2], ag_r.at[a, 2], e2).start()
        rc(ref, ref, ce_s.at[a, 1], ce_r.at[a, 1], (sib, z)).start()

    def g_step6(a):
        ref = res[a].at[own(c, q1, 1 - q2)]
        wait_recv(ref, ag_r.at[a, 1])
        rc(ref, ref, ce_s.at[a, 2], ce_r.at[a, 2], (sib, z)).start()
        ref = res[a].at[own(c, 1 - q1, 1 - q2)]
        wait_recv(ref, ag_r.at[a, 2])
        rc(ref, ref, ce_s.at[a, 3], ce_r.at[a, 3], (sib, z)).start()

    def g_end(a):
        lc(rb.at[a], res[a].at[own(c, q1, q2)], ag_l.at[a]).wait()
        o_ = 1 - c
        for k, rows in enumerate(
            (own(o_, q2, q1), own(o_, 1 - q2, q1), own(o_, q2, 1 - q1), own(o_, 1 - q2, 1 - q1))
        ):
            wait_recv(res[a].at[rows], ce_r.at[a, k])
            wait_send(rb.at[a], ce_s.at[a, k])
        for k in range(3):
            wait_send(rb.at[a], ag_s.at[a, k])
        for u in range(2):
            for r in range(2):
                wait_send(st1.at[a, u, r], g1_s.at[a, u, r])
                wait_send(st2.at[a, u, r], g2_s.at[a, u, r])

                @pl.when(jnp.logical_not((c == r) & (z == 2 * c + u)))
                def _(u=u, r=r):
                    wait_send(st2.at[a, u, r], g3_s.at[a, u, r])

    shared(dl, 1)

    for u in range(2):
        for n in range(3):
            cols = slice(768 * u + 256 * n, 768 * u + 256 * n + 256)
            g[2, u, 256 * n : 256 * n + 256, :] = mm(act[:, cols], dl[...], TN).astype(BF)
        g_start(2, u)

    def dup(t, _):
        u, cols = hidden(t)
        ub = jnp.zeros((1, 256), F32)
        for m in range(2):
            rr = slice(512 * m, 512 * m + 512)
            dv = mm(dl[rr, :], wg[2, u, cols, :], NT) * dg[rr, rows_of(t, 256)].astype(F32)
            dv = dv.astype(BF)
            dg[rr, rows_of(t, 256)] = dv
            ub = ub + jnp.sum(dv.astype(F32), axis=0, keepdims=True)
        vb[0, pl.ds(6 + 2 * c + u, 1), cols] = ub
        return 0

    for u in range(2):
        lax.fori_loop(3 * u, 3 * u + 3, dup, 0)
        for n in range(3):
            g[1, u, 256 * n : 256 * n + 256, :] = mm(
                flow[:, 256 * n : 256 * n + 256], dg[:, 768 * u : 768 * u + 768], TN
            ).astype(BF)
        g_start(1, u)
    partial(
        lambda rows, cols: mm(dg[rows, 0:768], wg[1, 0, cols, :], NT)
        + mm(dg[rows, 768:1536], wg[1, 1, cols, :], NT),
        2,
    )

    wait_send(dl.at[pl.ds(0, 512)], pe_s.at[5])
    def norm1b(m, carry):
        fg, fs, ob = carry
        rr = rows_of(m, 128)
        df = fst[rr, :] + op[rr, :] + rcv[2, rr, :].astype(F32)
        nv = n1[rr, :]
        gg = df * par[1:2, :]
        dr = (
            gg
            - jnp.mean(gg, axis=-1, keepdims=True)
            - nv * jnp.mean(gg * nv, axis=-1, keepdims=True)
        ) * rs1[rr, :]
        fst[rr, :] = dr
        dlo = dr.astype(BF)
        dl[at(mine, m, 128), :] = dlo
        return (
            fg + jnp.sum(df * nv, axis=0, keepdims=True),
            fs + jnp.sum(df, axis=0, keepdims=True),
            ob + jnp.sum(dlo.astype(F32), axis=0, keepdims=True),
        )

    fg, fs, ob = lax.fori_loop(0, 4, norm1b, (ones8, ones8, ones8))
    share(dl, 2)
    vb[0, 3:4, :] = fg
    vb[0, 4:5, :] = fs
    vb[0, 5:6, :] = ob
    shared(dl, 2)
    for u in range(2):
        g_step2(2, u)

    def dmix(m, _):
        rr = rows_of(m, 512)
        dm[rr, :] = mm(dl[rr, :], wo[...], NT).astype(BF)
        return 0

    lax.fori_loop(0, 2, dmix, 0)
    for i in range(3):
        gw = mm(mix[:, 128 * i : 128 * i + 128], dl[...], TN).astype(BF)
        for n, (u, rows) in enumerate((place(2 * i + 1, 3), place(2 * i, 3))):
            g[0, u, rows, :] = gw[64 * n : 64 * n + 64, :]

    def attend_back(i):
        for s in range(2):
            columns(2 * i + s, s)

        def body(t, _):
            rr = rows_of(t, 512)
            uu = []
            for s in range(2):
                w = mm(sort_mat(s, t), dm[:, 128 * i : 128 * i + 128])
                uu.append(
                    (jnp.where(low, 0.0, w) if s == 0 else jnp.where(low, w, 0.0)).astype(BF)
                )
            for s in range(2):
                kv = skv[2 * i + s, rr, :]
                q = sq[2 * i + s, rr, :]
                prob = pr[2 * i + s, rr, :]
                dp = jnp.concatenate(
                    [mm(piece(uu[s], k), piece(kv, k), NT) for k in four], axis=0
                )
                cen = jnp.sum(prob * dp, axis=-1, keepdims=True)
                ds = (prob * (dp - cen)).astype(BF)
                dq = jnp.concatenate([mm(piece(ds, k), piece(kv, k)) for k in four], axis=0) * 0.125
                pb = prob.astype(BF)
                dkv = jnp.concatenate(
                    [
                        mm(
                            jnp.concatenate([piece(pb, k), piece(ds, k)], axis=0),
                            jnp.concatenate([piece(uu[s], k), piece(q, k)], axis=0),
                            TN,
                        )
                        for k in four
                    ],
                    axis=0,
                ).astype(BF)
                if s == 0:
                    ms[s][rr, 0:128] = dkv
                    ms[s][rr, 128:256] = jnp.where(low, dq, 0.0).astype(BF)
                else:
                    ms[s][rr, 0:128] = jnp.where(low, 0.0, dq).astype(BF)
                    ms[s][rr, 128:256] = dkv
            return 0

        lax.fori_loop(0, 2, body, 0)

        def back(t, carry):
            ga = mm(unsort_mat(2 * i, t), ms[0][...])
            gb = mm(unsort_mat(2 * i + 1, t), ms[1][...])
            out = jnp.concatenate(
                [ga[:, 0:128], ga[:, 128:256] + gb[:, 0:128], gb[:, 128:256]], axis=1
            )
            qkv[rows_of(t, 512), 384 * i : 384 * i + 384] = out.astype(BF)
            return carry + jnp.sum(out, axis=0, keepdims=True)

        return lax.fori_loop(0, 2, back, jnp.zeros((1, 384), F32))

    def gqkv(i):
        gw = mm(qkv[:, 384 * i : 384 * i + 384], xall[...], TN).astype(BF)
        for k, (u, rows) in enumerate(pair_rows(i)):
            g[0, u, rows, :] = gw[64 * k : 64 * k + 64, :]

    b0 = attend_back(0)
    gqkv(0)
    for u in range(2):
        g_step3(2, u)
    b1 = attend_back(1)
    gqkv(1)
    g_start(0, 0)
    for u in range(2):
        g_step2(1, u)
    b2 = attend_back(2)
    gqkv(2)
    g_start(0, 1)
    for u in range(2):
        g_step3(1, u)
    bs = (b0, b1, b2)
    rest = jnp.zeros((1, 384), F32)
    for u in range(2):
        heads = range(3 * u, 3 * u + 3)
        qs = [bs[h // 2][:, 128 + 64 * (h % 2) : 192 + 64 * (h % 2)] for h in heads]
        vs = [bs[h // 2][:, 64 + 192 * (h % 2) : 128 + 192 * (h % 2)] for h in heads]
        vb[0, pl.ds(10 + 2 * c + u, 1), :] = jnp.concatenate(qs + vs + [rest], axis=1)

    vdev = (
        (sib, z), (xn, z), (yn, z), (d, z + 1 - 2 * zj), (d, z + 2 - 4 * zc),
    )

    def v_send(k):
        rc(vb.at[k], vr.at[k], v_s.at[k], v_r.at[k], vdev[k]).start()

    def v_add(k):
        wait_recv(vr.at[k], v_r.at[k])
        vb[k + 1] = vb[k] + vr[k]

    v_send(0)
    partial(
        lambda rows, cols: mm(qkv[rows, :], wq[:, cols]),
        3,
    )

    def gin(m, _):
        rr = rows_of(m, 128)
        gtok[rr, :] = (fst[rr, :] + op[rr, :] + rcv[3, rr, :].astype(F32)).astype(BF)
        return 0

    lax.fori_loop(0, 4, gin, 0)
    v_add(0)
    v_send(1)
    g_step2(0, 0)
    v_add(1)
    v_send(2)
    g_step3(0, 0)
    v_add(2)
    v_send(3)
    g_step2(0, 1)
    v_add(3)
    v_send(4)
    g_step3(0, 1)
    tok_send(gtok, o2, 1)
    g_step4(2)
    g_step4(1)
    g_step5(2)
    g_step5(1)
    g_step6(2)
    g_step6(1)
    g_step4(0)
    g_step5(0)
    v_add(4)
    vout[...] = vb[5]
    vout[14:15, :] = vb[5, pl.ds(6 + z, 1), :]
    vout[15:16, :] = vb[5, pl.ds(10 + z, 1), :]
    g_step6(0)
    for a in range(3):
        g_end(a)
    tok_wait(tok, o1, 0)
    tok_wait(gtok, o2, 1)

    for a in range(1, 3):
        w_end(a)
    for k in range(4):
        wait_send(xrows(k, c), cx_s.at[k])
        if k >= 2:
            wait_send(rcv.at[k], pe_s.at[k])
    for k in (0, 2):
        wait_send(flow.at[pl.ds(0, 512)], pe_s.at[4 + k])
    for k in range(5):
        wait_send(vb.at[k], v_s.at[k])
    for j in range(2):

        @pl.when(jnp.logical_not(prim & (z == 2 * c + j)))
        def _(j=j):
            wait_send(ord_in, o_s.at[j])

    @pl.when(prim)
    def _():
        for k in range(3):
            wait_send(bias_in, b_s.at[k])
        wait_send(mr_in, m_s.at[0])
        wait_send(mg_in, m_s.at[1])


def layer(x, order, wqkv, wout, wb, wc, mr, mg, *small):
    dma = pltpu.SemaphoreType.DMA
    hbm = pl.BlockSpec(memory_space=pl.ANY)
    vmem = pl.BlockSpec(memory_space=pltpu.VMEM)
    V = pltpu.VMEM
    return pl.pallas_call(
        kernel,
        out_shape=(
            jax.ShapeDtypeStruct((2, 256, 768), BF),
            jax.ShapeDtypeStruct((2, 256, 768), BF),
            jax.ShapeDtypeStruct((768, 768), BF),
            jax.ShapeDtypeStruct((768, 768), BF),
            jax.ShapeDtypeStruct((768, 768), BF),
            jax.ShapeDtypeStruct((16, 768), F32),
        ),
        in_specs=[hbm] * 8 + [vmem] * 8,
        out_specs=(hbm, hbm, hbm, hbm, hbm, vmem),
        scratch_shapes=[
            V((1024, 768), BF),
            V((256, 2, 768), BF),
            V((2, 3, 2, 1024), jnp.int32),
            V((3, 2, 768, 768), BF),
            V((2, 8, 768), F32),
            V((8, 768), F32),
            V((8, 768), F32),
            V(mr.shape, jnp.int32),
            V(mg.shape, BF),
            V((mg.shape[0], 768), BF),
            V((1152, 768), BF),
            V((384, 768), BF),
            V((1024, 1152), BF),
            V((2, 1024, 128), jnp.int32),
            V((6, 1024, 128), BF),
            V((6, 1024, 128), BF),
            V((6, 1024, 128), F32),
            V((1024, 384), BF),
            V((2, 512, 768), BF),
            V((4, 512, 768), BF),
            V((512, 768), F32),
            V((512, 768), F32),
            V((512, 768), F32),
            V((512, 1), F32),
            V((1024, 768), BF),
            V((1024, 1536), BF),
            V((1024, 1536), BF),
            V((1024, 768), BF),
            V((3, 2, 768, 768), BF),
            V((3, 2, 2, 192, 768), BF),
            V((3, 2, 2, 96, 768), BF),
            V((3, 4, 96, 768), BF),
            V((3, 96, 768), BF),
            V((6, 16, 768), F32),
            V((5, 16, 768), F32),
            dma((2, 2)), dma((4,)), dma, dma((4,)), dma((4,)),
            dma((2,)), dma((2,)), dma,
            dma((3,)), dma((2,)), dma,
            dma((2,)), dma((2,)), dma((2,)),
            dma((3, 2, 2)), dma((3, 2, 2)), dma((2, 2)), dma((3, 2, 2)),
            dma((3, 2, 2, 3)), dma((3, 2, 2, 3)), dma((4,)),
            dma((7,)), dma((7,)),
            dma((2, 2)), dma((2, 2)), dma((2,)),
            dma((5,)), dma((5,)),
            dma((3, 2, 2)), dma((3, 2, 2)), dma((3, 2, 2)), dma((3, 2, 2)),
            dma((3, 2, 2)), dma((3, 4)), dma((3, 3)), dma((3, 3)), dma((3,)),
            dma((3, 4)), dma((3, 4)),
        ],
        compiler_params=pltpu.CompilerParams(
            collective_id=0, has_side_effects=True, vmem_limit_bytes=60 * 2**20
        ),
    )(x, order, wqkv, wout, wb, wc, mr, mg, *small)


def finish_kernel(
    o1, o2, ra, rb, rc, vec, out, gin, gq, go, gb, gc, fg, fs, ob, db, sg, ss, ub, qv,
    o1v, o2v, rv, outv, ginv, gv, in_sem, out_sem,
):
    loads = [
        pltpu.make_async_copy(a, b, in_sem.at[k])
        for k, (a, b) in enumerate(
            ((o1, o1v), (o2, o2v), (ra, rv.at[0]), (rb, rv.at[1]), (rc, rv.at[2]))
        )
    ]
    for k in (2, 3, 4, 1, 0):
        loads[k].start()
    stores = [
        pltpu.make_async_copy(a, b, out_sem.at[k])
        for k, (a, b) in enumerate(
            (
                (gv.at[0, pl.ds(0, 576)], gq), (gv.at[0, pl.ds(576, 192)], go),
                (gv.at[1], gb), (gv.at[2], gc), (ginv, gin), (outv, out),
            )
        )
    ]
    for ref, row in ((sg, 0), (ss, 1), (db, 2), (fg, 3), (fs, 4), (ob, 5), (ub, 14)):
        ref[...] = vec[row, :]
    wide = qv.shape[1]
    qv[0:1, :] = vec[15:16, 0:wide]
    qv[1:2, :] = vec[15:16, wide : 2 * wide]

    for a in range(3):
        loads[2 + a].wait()

        def body(k, _, a=a):
            rr = pl.ds(pl.multiple_of(k * 96, 96), 96)
            gv[a, rr, :] = rv[a, rr, :].astype(F32)
            return 0

        lax.fori_loop(0, 8, body, 0)
        if a == 0:
            stores[0].start()
            stores[1].start()
        else:
            stores[a + 1].start()

    def weave(src, dst, dtype):
        def body(k, _):
            rr = pl.ds(pl.multiple_of(k * 32, 32), 32)
            both = jnp.stack([src[0, rr, :].astype(F32), src[1, rr, :].astype(F32)], axis=1)
            dst[rr] = both.astype(dtype)
            return 0

        lax.fori_loop(0, 8, body, 0)

    loads[1].wait()
    weave(o2v, ginv, F32)
    stores[4].start()
    loads[0].wait()
    weave(o1v, outv, BF)
    stores[5].start()
    for cp in stores:
        cp.wait()


def finish(o1, o2, ra, rb, rc, vec):
    hbm = pl.BlockSpec(memory_space=pl.ANY)
    vmem = pl.BlockSpec(memory_space=pltpu.VMEM)
    V = pltpu.VMEM
    S = jax.ShapeDtypeStruct
    row = S((768,), F32)
    return pl.pallas_call(
        finish_kernel,
        out_shape=(
            S((256, 2, 768), BF), S((256, 2, 768), F32), S((576, 768), F32), S((192, 768), F32),
            S((768, 768), F32), S((768, 768), F32), row, row, row, row, row, row, row,
            S((2, 192), F32),
        ),
        in_specs=[hbm] * 5 + [vmem],
        out_specs=(hbm,) * 6 + (vmem,) * 8,
        scratch_shapes=[
            V((2, 256, 768), BF), V((2, 256, 768), BF), V((3, 768, 768), BF),
            V((256, 2, 768), BF), V((256, 2, 768), F32), V((3, 768, 768), F32),
            pltpu.SemaphoreType.DMA((5,)), pltpu.SemaphoreType.DMA((6,)),
        ],
        compiler_params=pltpu.CompilerParams(vmem_limit_bytes=60 * 2**20),
    )(o1, o2, ra, rb, rc, vec)


def shards(
    inputs, qkv_weight, qv_bias, out_weight, out_bias, first_gain, first_shift,
    first_layer_weight, first_layer_bias, second_layer_weight, second_layer_bias,
    second_gain, second_shift, cluster_order, masked_rows, masked_grad,
):
    t = lax.axis_index("tensor")
    heads = qkv_weight.shape[2]
    wqkv = qkv_weight.transpose(1, 2, 0).reshape(3 * heads, 768)
    order = cluster_order.transpose(1, 0, 2)

    o1, o2, ra, rb, rc, vec = layer(
        inputs, order, wqkv, out_weight, first_layer_weight, second_layer_weight,
        masked_rows, masked_grad.transpose(1, 0, 2), qv_bias,
        out_bias, first_gain, first_shift, second_layer_bias, second_gain, second_shift,
        first_layer_bias,
    )

    many = lax.axis_size("dp") // 8
    if many > 1:
        groups = [[8 * i + j for i in range(many)] for j in range(8)]
        ra, rb, rc = lax.psum(
            (ra.astype(F32), rb.astype(F32), rc.astype(F32)), "dp", axis_index_groups=groups
        )
        ra, rb, rc = ra.astype(BF), rb.astype(BF), rc.astype(BF)
        vec = lax.psum(vec, "dp", axis_index_groups=groups)
    outputs, grad_inputs, gq, go, gb, gc, fg, fs, ob, db, sg, ss, ub, qv = finish(
        o1, o2, ra, rb, rc, vec
    )
    return (
        outputs,
        grad_inputs,
        gq.reshape(3, heads, 768).transpose(2, 0, 1),
        qv,
        go,
        ob,
        fg,
        fs,
        gb,
        ub,
        gc,
        db,
        sg,
        ss,
    )


def solution(mesh):
    placed = (
        P("tensor", "dp", None), P(None, None, "tensor"), P(None, "tensor"), P("tensor", None),
        P(), P(), P(), P(None, "tensor"), P("tensor"), P("tensor", None), P(), P(), P(),
        P("dp", "tensor", None), P("dp", None), P("dp", None, None),
    )
    return jax.shard_map(
        shards,
        mesh=mesh,
        in_specs=placed,
        out_specs=(
            P("tensor", "dp", None), P("tensor", "dp", None), P(None, None, "tensor"),
            P(None, "tensor"), P("tensor", None), P(), P(), P(), P(None, "tensor"), P("tensor"),
            P("tensor", None), P(), P(), P(),
        ),
        check_vma=False,
    )
```

```python
import math

import jax
import jax.numpy as jnp
from jax import lax
from jax.experimental import pallas as pl
from jax.experimental.pallas import tpu as pltpu
from jax.sharding import PartitionSpec as P

HD = 64
C = 128
NORM_EPS = 1e-05
BF = jnp.bfloat16
F32 = jnp.float32
MESH = pl.DeviceIdType.MESH
DIRECT = (2,)
RSQRT2 = 1.0 / math.sqrt(2.0)
RSQRT2PI = 1.0 / math.sqrt(2.0 * math.pi)

NN = (((1,), (0,)), ((), ()))
NT = (((1,), (1,)), ((), ()))
TN = (((0,), (0,)), ((), ()))


def mm(a, b, dims=NN):
    return lax.dot_general(a, b, dims, preferred_element_type=F32)


def kernel(
    x_in, ord_in, wq_in, wo_in, wb_in, wc_in, mr_in, mg_in, qb_in,
    p0, p1_, p2_, p3_, p4_, p5_, p6_,
    o1, o2, ra, rbb, rcc, vout,
    xall, x3, ordv, wg, bias, bias_in, par, mr, mg3, mg, wq, wo, qkv, oc, sq, skv, pr, mix,
    snd, rcv, op, fst, n1, rs1, flow, act, dg, dl, g, st1, st2, st3,
    rb, vb, vr,
    x_s, x_r, x_l, cx_s, cx_r, o_s, o_r, o_l, b_s, b_r, b_l, m_s, m_r, m_l,
    wz_s, wz_s2, wz_s3, wz_r, wx_s, wx_r, w_l, pe_s, pe_r, sh_s, sh_r, t_s, t_r, t_l, v_s, v_r,
    g1_s, g1_r, g2_s, g2_r, g3_s, g3_r, ag_s, ag_r, ag_l, ce_s, ce_r,
):
    w_in = (None, wb_in, wc_in)
    res = (ra, rbb, rcc)
    dm = act.at[:, 0:384]
    ms = (act.at[:, 512:768], act.at[:, 768:1024])
    tok = wg.at[0, 0, pl.ds(0, 512)]
    gtok = wg.at[0, 1, pl.ds(0, 512)]
    d = lax.axis_index("dp")
    z = lax.axis_index("tensor")
    c = lax.rem(d, 2)
    base = d - c
    sib = base + 1 - c
    px = lax.rem(lax.div(d, 2), 2)
    py = lax.rem(lax.div(d, 4), 2)
    xn = d + 2 - 4 * px
    yn = d + 4 - 8 * py
    zc = lax.div(z, 2)
    zj = lax.rem(z, 2)
    up = 1 - 2 * c
    zz = 3 * c + z * up
    prim = zc == c

    def rc(src, dst, ss, rs, dev):
        return pltpu.make_async_remote_copy(
            src_ref=src, dst_ref=dst, send_sem=ss, recv_sem=rs,
            device_id=dev, device_id_type=MESH,
        )

    def wait_send(src, ss):
        rc(src, src, ss, ss, (sib, z)).wait_send()

    def wait_recv(dst, rs):
        rc(dst, dst, rs, rs, (sib, z)).wait_recv()

    def lc(src, dst, sem):
        return pltpu.make_async_copy(src, dst, sem)

    bar = pltpu.get_barrier_semaphore()
    for k in range(1, 8):
        oc_, oz = k % 2, k // 2
        dev = (base + lax.rem(c + oc_, 2), lax.rem(z + oz, 4))
        pl.semaphore_signal(bar, inc=1, device_id=dev, device_id_type=MESH)
    for dev in ((xn, z), (yn, z)):
        pl.semaphore_signal(bar, inc=1, device_id=dev, device_id_type=MESH)
    pl.semaphore_wait(bar, 9)

    def pp(r):
        return (px, py) if r == 0 else (py, px)

    def nbs(r):
        return ((xn, z), (yn, z)) if r == 0 else ((yn, z), (xn, z))

    def blk(r, p1, p2):
        return pl.ds(pl.multiple_of(384 * r + 96 * (2 * p1 + p2), 32), 96)

    def uof(v):
        return c + v * up

    def w_start(a):
        for v in range(2):
            for r in range(2):
                p1, p2 = pp(r)
                rows = blk(r, p1, p2)
                dst = wg.at[a, uof(v), rows]
                if a > 0:
                    parts = ((zz == v, w_in[a].at[rows]),)
                elif r == 0:
                    parts = ((zz == v, wq_in.at[rows]),)
                else:
                    off = pl.ds(pl.multiple_of(96 * p2, 32), 96)
                    high = pl.ds(pl.multiple_of(384 + 96 * p2, 32), 96)
                    parts = (
                        ((zz == v) & (p1 == 0), wq_in.at[high]),
                        ((zz == v) & (p1 == 1), wo_in.at[off]),
                    )
                near = z + up if v == 0 else z - up
                far = z + 2 * up if v == 0 else z + up
                last = z + (3 - v) * up
                for cond, src in parts:

                    @pl.when(cond)
                    def _(src=src, dst=dst, v=v, r=r, near=near, far=far, last=last):
                        rc(src, dst, wz_s.at[a, v, r], wz_r.at[a, v, r], (d, near)).start()
                        rc(src, dst, wz_s2.at[a, v, r], wz_r.at[a, v, r], (d, far)).start()
                        if a in DIRECT:
                            rc(src, dst, wz_s3.at[v, r], wz_r.at[a, v, r], (d, last)).start()

    def w_copies(a, v):
        if a > 0:
            return (lc(w_in[a], wg.at[a, uof(v)], w_l.at[a]),)
        return (
            lc(wq_in, wg.at[0, uof(v), pl.ds(0, 576)], w_l.at[0]),
            lc(wo_in, wg.at[0, uof(v), pl.ds(576, 192)], w_l.at[3]),
        )

    def w_local(a):
        for v in range(2):

            @pl.when(zz == v)
            def _(v=v):
                for cp in w_copies(a, v):
                    cp.start()

    def w_fwd(a, stage):
        for v in range(2):
            for r in range(2):
                p1, p2 = pp(r)
                ref = wg.at[a, uof(v), blk(r, p1, p2)]
                n1_, n2_ = nbs(r)
                cond = (zz == 3) if stage else ((zz == 1 - v) | (zz == 2))
                if a in DIRECT:
                    cond = zz != v

                @pl.when(cond)
                def _(ref=ref, v=v, r=r, n1_=n1_, n2_=n2_):
                    wait_recv(ref, wz_r.at[a, v, r])
                    rc(ref, ref, wx_s.at[a, v, r, 0], wx_r.at[a, v, r, 0], n1_).start()
                    rc(ref, ref, wx_s.at[a, v, r, 1], wx_r.at[a, v, r, 1], n2_).start()

                if not stage and a not in DIRECT:

                    @pl.when(zz == 2)
                    def _(ref=ref, v=v, r=r):
                        rc(ref, ref, wz_s.at[a, v, r], wz_r.at[a, v, r], (d, z + up)).start()

    def w_fwd2(a):
        for v in range(2):
            for r in range(2):
                p1, p2 = pp(r)
                ref = wg.at[a, uof(v), blk(r, 1 - p1, p2)]
                n1_, n2_ = nbs(r)

                @pl.when(zz != v)
                def _(ref=ref, v=v, r=r, n2_=n2_):
                    wait_recv(ref, wx_r.at[a, v, r, 0])
                    rc(ref, ref, wx_s.at[a, v, r, 2], wx_r.at[a, v, r, 2], n2_).start()

    def w_done(a):
        for v in range(2):
            for r in range(2):
                p1, p2 = pp(r)

                @pl.when(zz != v)
                def _(v=v, r=r, p1=p1, p2=p2):
                    wait_recv(wg.at[a, uof(v), blk(r, p1, 1 - p2)], wx_r.at[a, v, r, 1])
                    wait_recv(wg.at[a, uof(v), blk(r, 1 - p1, 1 - p2)], wx_r.at[a, v, r, 2])

            @pl.when(zz == v)
            def _(v=v):
                for cp in w_copies(a, v):
                    cp.wait()

    def w_end(a):
        for v in range(2):
            for r in range(2):
                p1, p2 = pp(r)
                ref = wg.at[a, uof(v), blk(r, p1, p2)]

                @pl.when((zz == v) if a in DIRECT else ((zz == v) | (zz == 2)))
                def _(ref=ref, v=v, r=r):
                    wait_send(ref, wz_s.at[a, v, r])

                @pl.when(zz == v)
                def _(ref=ref, v=v, r=r):
                    wait_send(ref, wz_s2.at[a, v, r])
                    if a in DIRECT:
                        wait_send(ref, wz_s3.at[v, r])

                @pl.when(zz != v)
                def _(ref=ref, v=v, r=r):
                    for k in range(3):
                        wait_send(ref, wx_s.at[a, v, r, k])

    w_start(0)
    w_local(0)
    lc(x_in, x3, x_l).start()
    for k, ref in enumerate((p0, p1_, p2_, p3_, p4_, p5_)):
        par[k : k + 1, :] = ref[...].astype(F32).reshape(1, 768)
    bias_in[...] = jnp.zeros((8, 768), F32)
    bias_in[0:2, 0:192] = qb_in[...].astype(F32)
    bias_in[2:3, :] = p6_[...].astype(F32).reshape(1, 768)

    for j in range(2):
        dev = (base + zc, 2 * c + j)
        self_ = (zc == c) & (z == 2 * c + j)

        @pl.when(self_)
        def _(j=j):
            lc(ord_in, ordv.at[zj], o_l).start()

        @pl.when(jnp.logical_not(self_))
        def _(j=j, dev=dev):
            rc(ord_in, ordv.at[lax.rem(z, 2)], o_s.at[j], o_r.at[zj], dev).start()

    @pl.when(prim)
    def _():
        for k in range(1, 4):
            dev = (d, lax.rem(z + k, 4))
            rc(bias_in, bias.at[zj], b_s.at[k - 1], b_r.at[zj], dev).start()
        lc(bias_in, bias.at[zj], b_l).start()
        lc(mr_in, mr, m_l.at[0]).start()
        lc(mg_in, mg3, m_l.at[1]).start()
        rc(mr_in, mr, m_s.at[0], m_r.at[0], (sib, z)).start()
        rc(mg_in, mg3, m_s.at[1], m_r.at[1], (sib, z)).start()


    w_local(1)
    w_local(2)
    lc(x_in, x3, x_l).wait()

    def part(k, _):
        both = x3[pl.ds(pl.multiple_of(32 * k, 32), 32)].astype(F32)
        for j in range(2):
            dg[pl.ds(pl.multiple_of(256 * j + 32 * k, 32), 32), 0:768] = both[:, j, :].astype(BF)
        return 0

    lax.fori_loop(0, 8, part, 0)
    for j in range(2):
        for h in range(2):
            zt = 2 * c + j
            rows = pl.ds(128 * h, 128)
            self_ = (c == h) & (z == zt)
            src = dg.at[pl.ds(256 * j + 128 * h, 128), 0:768]
            dst = xall.at[pl.ds(pl.multiple_of(256 * z + 128 * h, 128), 128)]

            @pl.when(self_)
            def _(src=src, dst=dst):
                lc(src, dst, x_l).start()

            @pl.when(jnp.logical_not(self_))
            def _(src=src, dst=dst, j=j, h=h, zt=zt):
                rc(src, dst, x_s.at[j, h], x_r.at[z], (base + h, zt)).start()

    w_fwd(0, 0)
    w_fwd(0, 1)
    w_fwd2(0)

    def xrows(k, h):
        return xall.at[pl.ds(pl.multiple_of(256 * k + 128 * h, 128), 128)]

    for u in range(2):
        loc = prim & (zj == u)

        @pl.when(loc)
        def _(u=u):
            lc(ord_in, ordv.at[u], o_l).wait()
            lc(bias_in, bias.at[u], b_l).wait()

        @pl.when(jnp.logical_not(loc))
        def _(u=u):
            wait_recv(ordv.at[u], o_r.at[u])
            wait_recv(bias.at[u], b_r.at[u])

    @pl.when(prim)
    def _():
        lc(mr_in, mr, m_l.at[0]).wait()
        lc(mg_in, mg3, m_l.at[1]).wait()

    @pl.when(jnp.logical_not(prim))
    def _():
        wait_recv(mr, m_r.at[0])
        wait_recv(mg3, m_r.at[1])

    both = mg3[...].astype(F32)
    mg[...] = jnp.where(zj == 0, both[:, 0, :], both[:, 1, :]).astype(BF)
    w_done(0)

    lane = lax.broadcasted_iota(jnp.int32, (512, 128), 1)
    sub = lax.broadcasted_iota(jnp.int32, (512, 1024), 0)
    low = lane < 64

    def place(h, kind):
        return h // 3, slice(192 * kind + 64 * (h % 3), 192 * kind + 64 * (h % 3) + 64)

    def pair_rows(i):
        a, b = 2 * i, 2 * i + 1
        return (place(a, 1), place(a, 2), place(a, 0), place(b, 0), place(b, 2), place(b, 1))

    for i in range(3):
        for n, (u, rows) in enumerate(pair_rows(i)):
            wq[384 * i + 64 * n : 384 * i + 64 * n + 64, :] = wg[0, u, rows, :]
        for n, (u, rows) in enumerate((place(2 * i + 1, 3), place(2 * i, 3))):
            wo[128 * i + 64 * n : 128 * i + 64 * n + 64, :] = wg[0, u, rows, :]

    for k in range(4):
        ref = xrows(k, c)
        loc = prim & (z == k)

        @pl.when(loc)
        def _(ref=ref):
            lc(ref, ref, x_l).wait()

        @pl.when(jnp.logical_not(loc))
        def _(ref=ref, k=k):
            wait_recv(ref, x_r.at[k])

        rc(ref, ref, cx_s.at[k], cx_r.at[k], (sib, z)).start()
    w_start(1)
    for k in range(4):
        wait_recv(xrows(k, 1 - c), cx_r.at[k])

    def bq(i):
        nil = jnp.zeros((1, 64), F32)

        def take(h, row):
            return bias[h // 3, row : row + 1, 64 * (h % 3) : 64 * (h % 3) + 64]

        a, b = 2 * i, 2 * i + 1
        return jnp.concatenate(
            [nil, take(a, 1), take(a, 0), take(b, 0), take(b, 1), nil], axis=1
        )

    def rows_of(m, n):
        return pl.ds(pl.multiple_of(m * n, n), n)

    for lo_, hi_ in ((0, 2), (2, 3)):
        bv = jnp.concatenate([bq(i) for i in range(lo_, hi_)], axis=1)
        cols = slice(384 * lo_, 384 * hi_)

        def body(k, _, cols=cols, bv=bv):
            rr = rows_of(k, 512)
            qkv[rr, cols] = (mm(xall[rr, :], wq[cols, :], NT) + bv).astype(BF)
            return 0

        lax.fori_loop(0, 2, body, 0)

    w_fwd(1, 0)
    w_start(2)

    def columns(h, s):
        row = ordv[h // 3, h % 3, pl.ds(zj, 1), :]
        oc[s] = jnp.broadcast_to(row, (128, 1024)).T

    def sort_mat(s, t):
        b = oc[s, rows_of(t, 512), :]
        return jnp.concatenate(
            [jnp.where(b == lane + 128 * k, 1.0, 0.0).astype(BF) for k in range(8)], axis=1
        )

    def unsort_mat(h, t):
        row = ordv[h // 3, h % 3, pl.ds(zj, 1), :]
        return jnp.where(sub + 512 * t == row, 1.0, 0.0).astype(BF)

    four = range(4)

    def piece(w, k):
        return w[128 * k : 128 * k + 128]

    def attend(i):
        for s in range(2):
            columns(2 * i + s, s)

        def body(t, _):
            rr = rows_of(t, 512)
            q, kv = [], []
            for s in range(2):
                at_ = 384 * i + 128 * s
                w = mm(sort_mat(s, t), qkv[:, at_ : at_ + 256])
                if s == 0:
                    kv.append(w[:, 0:128].astype(BF))
                    q.append((jnp.where(low, w[:, 128:256], 0.0) * 0.125).astype(BF))
                else:
                    q.append((jnp.where(low, 0.0, w[:, 0:128]) * 0.125).astype(BF))
                    kv.append(w[:, 128:256].astype(BF))
                sq[2 * i + s, rr, :] = q[s]
                skv[2 * i + s, rr, :] = kv[s]
            for s in range(2):
                sc = [mm(piece(q[s], k), piece(kv[s], k), NT) for k in four]
                sc = jnp.concatenate(sc, axis=0)
                ex = jnp.exp(sc - jnp.max(sc, axis=-1, keepdims=True))
                prob = ex * (1.0 / jnp.sum(ex, axis=-1, keepdims=True))
                pr[2 * i + s, rr, :] = prob
                pb = prob.astype(BF)
                mx = jnp.concatenate([mm(piece(pb, k), piece(kv[s], k)) for k in four], axis=0)
                keep = jnp.where(low, 0.0, mx) if s == 0 else jnp.where(low, mx, 0.0)
                ms[s][rr, 0:128] = keep.astype(BF)
            return 0

        lax.fori_loop(0, 2, body, 0)

        def back(t, _):
            both = mm(unsort_mat(2 * i, t), ms[0][:, 0:128]) + mm(
                unsort_mat(2 * i + 1, t), ms[1][:, 0:128]
            )
            mix[rows_of(t, 512), 128 * i : 128 * i + 128] = both.astype(BF)
            return 0

        lax.fori_loop(0, 2, back, 0)

    attend(0)
    w_fwd(1, 1)
    attend(1)
    w_fwd2(1)
    w_fwd(2, 0)
    attend(2)

    mine = 512 * c
    other = 512 - mine

    def at(off, m, n):
        return pl.ds(pl.multiple_of(off + m * n, n), n)

    def partial(fn, k):
        if k >= 2:
            wait_send(snd.at[k % 2], pe_s.at[k - 2])
        for n in range(3):
            cols = slice(256 * n, 256 * n + 256)
            snd[k % 2, :, cols] = fn(at(other, 0, 512), cols).astype(BF)
        rc(snd.at[k % 2], rcv.at[k], pe_s.at[k], pe_r.at[k], (sib, z)).start()
        for n in range(3):
            cols = slice(256 * n, 256 * n + 256)
            op[:, cols] = fn(at(mine, 0, 512), cols)
        wait_recv(rcv.at[k], pe_r.at[k])

    def share(ref, k):
        own = ref.at[pl.ds(pl.multiple_of(mine, 512), 512)]
        rc(own, own, pe_s.at[4 + k], pe_r.at[4 + k], (sib, z)).start()

    def shared(ref, k):
        wait_recv(ref.at[pl.ds(pl.multiple_of(other, 512), 512)], pe_r.at[4 + k])

    partial(lambda rows, cols: mm(mix[rows, :], wo[:, cols]), 0)

    def norm1(m, _):
        rr = rows_of(m, 128)
        v = (
            xall[at(mine, m, 128), :].astype(F32)
            + op[rr, :]
            + rcv[0, rr, :].astype(F32)
            + par[0:1, :]
        )
        cen = v - jnp.mean(v, axis=-1, keepdims=True)
        rstd = lax.rsqrt(jnp.mean(cen * cen, axis=-1, keepdims=True) + NORM_EPS)
        nv = cen * rstd
        n1[rr, :] = nv
        rs1[rr, :] = rstd
        fv = nv * par[1:2, :] + par[2:3, :]
        fst[rr, :] = fv
        flow[at(mine, m, 128), :] = fv.astype(BF)
        return 0

    lax.fori_loop(0, 4, norm1, 0)
    share(flow, 0)
    w_done(1)

    for j in range(2):
        for h in range(2):

            @pl.when(jnp.logical_not((c == h) & (z == 2 * c + j)))
            def _(j=j, h=h):
                wait_send(dg.at[pl.ds(0, 128), 0:768], x_s.at[j, h])

    def hidden(t):
        return lax.div(t, 3), rows_of(lax.rem(t, 3), 256)

    def ffn_up(off):
        def body(t, _):
            u, cols = hidden(t)
            rr = at(off, 0, 512)
            h = mm(flow[rr, :], wg[1, u, :, cols]) + bias[u, 2:3, cols]
            cdf = 0.5 + 0.5 * lax.erf(h * RSQRT2)
            act[rr, rows_of(t, 256)] = (h * cdf).astype(BF)
            dg[rr, rows_of(t, 256)] = (cdf + h * (jnp.exp(-0.5 * h * h) * RSQRT2PI)).astype(BF)
            return 0

        lax.fori_loop(0, 6, body, 0)

    ffn_up(mine)
    w_fwd2(2)
    shared(flow, 0)
    ffn_up(other)
    w_done(2)
    partial(
        lambda rows, cols: mm(act[rows, 0:768], wg[2, 0, :, cols])
        + mm(act[rows, 768:1536], wg[2, 1, :, cols]),
        1,
    )

    w_end(0)

    vb[0] = jnp.zeros((16, 768), F32)
    ones8 = jnp.zeros((1, 768), F32)

    def norm2(m, carry):
        sgain, sshift, dbias = carry
        rr = rows_of(m, 128)
        v = fst[rr, :] + op[rr, :] + rcv[1, rr, :].astype(F32) + par[3:4, :]
        cen = v - jnp.mean(v, axis=-1, keepdims=True)
        rstd = lax.rsqrt(jnp.mean(cen * cen, axis=-1, keepdims=True) + NORM_EPS)
        nv = cen * rstd
        tok[rr, :] = (nv * par[4:5, :] + par[5:6, :]).astype(BF)
        pos = lax.broadcasted_iota(jnp.int32, (128, mr.shape[1]), 0) + (mine + 128 * m)
        hits = jnp.where(pos == mr[pl.ds(zj, 1), :], 1.0, 0.0).astype(BF)
        dout = mm(hits, mg[...])
        gg = dout * par[4:5, :]
        d2 = (
            gg
            - jnp.mean(gg, axis=-1, keepdims=True)
            - nv * jnp.mean(gg * nv, axis=-1, keepdims=True)
        ) * rstd
        fst[rr, :] = d2
        dlo = d2.astype(BF)
        dl[at(mine, m, 128), :] = dlo
        piece_ = dl.at[at(mine, m, 128)]
        rc(piece_, piece_, sh_s.at[m], sh_r.at[m], (sib, z)).start()
        return (
            sgain + jnp.sum(dout * nv, axis=0, keepdims=True),
            sshift + jnp.sum(dout, axis=0, keepdims=True),
            dbias + jnp.sum(dlo.astype(F32), axis=0, keepdims=True),
        )

    sg, ss, db = lax.fori_loop(0, 4, norm2, (ones8, ones8, ones8))
    vb[0, 0:1, :] = sg
    vb[0, 1:2, :] = ss
    vb[0, 2:3, :] = db

    def tok_send(src, dst, k):
        for u in range(2):
            self_ = prim & (z == 2 * c + u)
            s_ = src.at[pl.ds(256 * u, 256)]
            d_ = dst.at[zj]

            @pl.when(self_)
            def _(s_=s_, d_=d_):
                lc(s_, d_, t_l.at[k]).start()

            @pl.when(jnp.logical_not(self_))
            def _(s_=s_, d_=d_, u=u):
                rc(s_, d_, t_s.at[k, u], t_r.at[k, zj], (base + zc, 2 * c + u)).start()

    def tok_wait(src, dst, k):
        for j in range(2):
            loc = prim & (z == 2 * c + j)

            @pl.when(loc)
            def _(j=j):
                lc(src.at[pl.ds(0, 256)], dst.at[j], t_l.at[k]).wait()

            @pl.when(jnp.logical_not(loc))
            def _(j=j):
                wait_recv(dst.at[j], t_r.at[k, j])
                wait_send(src.at[pl.ds(0, 256)], t_s.at[k, j])

    tok_send(tok, o1, 0)

    def g_start(a, u):
        for r in range(2):
            p1, p2 = pp(r)
            src = g.at[a, u, pl.ds(pl.multiple_of(384 * r + 192 * (1 - p1), 64), 192)]
            rc(src, st1.at[a, u, r], g1_s.at[a, u, r], g1_r.at[a, u, r], nbs(r)[0]).start()

    def quarter(ref, r, q):
        return ref.at[pl.ds(pl.multiple_of(96 * q, 32), 96)]

    def g_step2(a, u):
        for r in range(2):
            p1, p2 = pp(r)
            wait_recv(st1.at[a, u, r], g1_r.at[a, u, r])
            rows = blk(r, p1, 1 - p2)
            part = st1[a, u, r, pl.ds(pl.multiple_of(96 * (1 - p2), 32), 96), :]
            g[a, u, rows, :] = (g[a, u, rows, :].astype(F32) + part.astype(F32)).astype(BF)
            rc(
                g.at[a, u, rows], st2.at[a, u, r], g2_s.at[a, u, r], g2_r.at[a, u, r], nbs(r)[1]
            ).start()

    def g_step3(a, u):
        for r in range(2):
            p1, p2 = pp(r)
            wait_recv(st2.at[a, u, r], g2_r.at[a, u, r])
            rows = blk(r, p1, p2)
            part = st1[a, u, r, pl.ds(pl.multiple_of(96 * p2, 32), 96), :]
            tot = (
                g[a, u, rows, :].astype(F32) + part.astype(F32) + st2[a, u, r].astype(F32)
            ).astype(BF)
            self_ = (c == r) & (z == 2 * c + u)

            @pl.when(self_)
            def _(tot=tot):
                st3[a, z] = tot

            @pl.when(jnp.logical_not(self_))
            def _(tot=tot, rows=rows, r=r):
                g[a, u, rows, :] = tot
                rc(
                    g.at[a, u, rows], st3.at[a, z], g3_s.at[a, u, r], g3_r.at[a, z],
                    (base + r, 2 * c + u),
                ).start()

    q1 = px + c * (py - px)
    q2 = py + c * (px - py)
    e1 = (xn + c * (yn - xn), z)
    e2 = (yn + c * (xn - yn), z)

    def own(r, p1, p2):
        return pl.ds(pl.multiple_of(384 * r + 96 * (2 * p1 + p2), 32), 96)

    def g_step4(a):
        for k in range(4):
            loc = prim & (z == k)

            @pl.when(jnp.logical_not(loc))
            def _(k=k):
                wait_recv(st3.at[a, k], g3_r.at[a, k])

        rb[a] = (
            st3[a, 0].astype(F32)
            + st3[a, 1].astype(F32)
            + st3[a, 2].astype(F32)
            + st3[a, 3].astype(F32)
        ).astype(BF)
        dst = res[a].at[own(c, q1, q2)]
        rc(rb.at[a], dst, ag_s.at[a, 0], ag_r.at[a, 0], e1).start()
        rc(rb.at[a], dst, ag_s.at[a, 1], ag_r.at[a, 1], e2).start()
        rc(rb.at[a], dst, ce_s.at[a, 0], ce_r.at[a, 0], (sib, z)).start()
        lc(rb.at[a], dst, ag_l.at[a]).start()

    def g_step5(a):
        ref = res[a].at[own(c, 1 - q1, q2)]
        wait_recv(ref, ag_r.at[a, 0])
        rc(ref, ref, ag_s.at[a, 2], ag_r.at[a, 2], e2).start()
        rc(ref, ref, ce_s.at[a, 1], ce_r.at[a, 1], (sib, z)).start()

    def g_step6(a):
        ref = res[a].at[own(c, q1, 1 - q2)]
        wait_recv(ref, ag_r.at[a, 1])
        rc(ref, ref, ce_s.at[a, 2], ce_r.at[a, 2], (sib, z)).start()
        ref = res[a].at[own(c, 1 - q1, 1 - q2)]
        wait_recv(ref, ag_r.at[a, 2])
        rc(ref, ref, ce_s.at[a, 3], ce_r.at[a, 3], (sib, z)).start()

    def g_end(a):
        lc(rb.at[a], res[a].at[own(c, q1, q2)], ag_l.at[a]).wait()
        o_ = 1 - c
        for k, rows in enumerate(
            (own(o_, q2, q1), own(o_, 1 - q2, q1), own(o_, q2, 1 - q1), own(o_, 1 - q2, 1 - q1))
        ):
            wait_recv(res[a].at[rows], ce_r.at[a, k])
            wait_send(rb.at[a], ce_s.at[a, k])
        for k in range(3):
            wait_send(rb.at[a], ag_s.at[a, k])
        for u in range(2):
            for r in range(2):
                wait_send(st1.at[a, u, r], g1_s.at[a, u, r])
                wait_send(st2.at[a, u, r], g2_s.at[a, u, r])

                @pl.when(jnp.logical_not((c == r) & (z == 2 * c + u)))
                def _(u=u, r=r):
                    wait_send(st2.at[a, u, r], g3_s.at[a, u, r])

    for m in range(4):
        wait_recv(dl.at[at(other, m, 128)], sh_r.at[m])

    for u in range(2):
        for n in range(3):
            cols = slice(768 * u + 256 * n, 768 * u + 256 * n + 256)
            g[2, u, 256 * n : 256 * n + 256, :] = mm(act[:, cols], dl[...], TN).astype(BF)
        g_start(2, u)

    def dup(t, _):
        u, cols = hidden(t)
        ub = jnp.zeros((1, 256), F32)
        for m in range(2):
            rr = slice(512 * m, 512 * m + 512)
            dv = mm(dl[rr, :], wg[2, u, cols, :], NT) * dg[rr, rows_of(t, 256)].astype(F32)
            dv = dv.astype(BF)
            dg[rr, rows_of(t, 256)] = dv
            ub = ub + jnp.sum(dv.astype(F32), axis=0, keepdims=True)
        vb[0, pl.ds(6 + 2 * c + u, 1), cols] = ub
        return 0

    for u in range(2):
        lax.fori_loop(3 * u, 3 * u + 3, dup, 0)
        for n in range(3):
            g[1, u, 256 * n : 256 * n + 256, :] = mm(
                flow[:, 256 * n : 256 * n + 256], dg[:, 768 * u : 768 * u + 768], TN
            ).astype(BF)
        g_start(1, u)
    partial(
        lambda rows, cols: mm(dg[rows, 0:768], wg[1, 0, cols, :], NT)
        + mm(dg[rows, 768:1536], wg[1, 1, cols, :], NT),
        2,
    )

    for m in range(4):
        wait_send(dl.at[pl.ds(0, 128)], sh_s.at[m])
    def norm1b(m, carry):
        fg, fs, ob = carry
        rr = rows_of(m, 128)
        df = fst[rr, :] + op[rr, :] + rcv[2, rr, :].astype(F32)
        nv = n1[rr, :]
        gg = df * par[1:2, :]
        dr = (
            gg
            - jnp.mean(gg, axis=-1, keepdims=True)
            - nv * jnp.mean(gg * nv, axis=-1, keepdims=True)
        ) * rs1[rr, :]
        fst[rr, :] = dr
        dlo = dr.astype(BF)
        dl[at(mine, m, 128), :] = dlo
        return (
            fg + jnp.sum(df * nv, axis=0, keepdims=True),
            fs + jnp.sum(df, axis=0, keepdims=True),
            ob + jnp.sum(dlo.astype(F32), axis=0, keepdims=True),
        )

    fg, fs, ob = lax.fori_loop(0, 4, norm1b, (ones8, ones8, ones8))
    share(dl, 2)
    vb[0, 3:4, :] = fg
    vb[0, 4:5, :] = fs
    vb[0, 5:6, :] = ob
    shared(dl, 2)
    for u in range(2):
        g_step2(2, u)

    def dmix(m, _):
        rr = rows_of(m, 512)
        dm[rr, :] = mm(dl[rr, :], wo[...], NT).astype(BF)
        return 0

    lax.fori_loop(0, 2, dmix, 0)
    for i in range(3):
        gw = mm(mix[:, 128 * i : 128 * i + 128], dl[...], TN).astype(BF)
        for n, (u, rows) in enumerate((place(2 * i + 1, 3), place(2 * i, 3))):
            g[0, u, rows, :] = gw[64 * n : 64 * n + 64, :]

    def attend_back(i):
        for s in range(2):
            columns(2 * i + s, s)

        def body(t, _):
            rr = rows_of(t, 512)
            uu = []
            for s in range(2):
                w = mm(sort_mat(s, t), dm[:, 128 * i : 128 * i + 128])
                uu.append(
                    (jnp.where(low, 0.0, w) if s == 0 else jnp.where(low, w, 0.0)).astype(BF)
                )
            for s in range(2):
                kv = skv[2 * i + s, rr, :]
                q = sq[2 * i + s, rr, :]
                prob = pr[2 * i + s, rr, :]
                dp = jnp.concatenate(
                    [mm(piece(uu[s], k), piece(kv, k), NT) for k in four], axis=0
                )
                cen = jnp.sum(prob * dp, axis=-1, keepdims=True)
                ds = (prob * (dp - cen)).astype(BF)
                dq = jnp.concatenate([mm(piece(ds, k), piece(kv, k)) for k in four], axis=0) * 0.125
                pb = prob.astype(BF)
                dkv = jnp.concatenate(
                    [
                        mm(
                            jnp.concatenate([piece(pb, k), piece(ds, k)], axis=0),
                            jnp.concatenate([piece(uu[s], k), piece(q, k)], axis=0),
                            TN,
                        )
                        for k in four
                    ],
                    axis=0,
                ).astype(BF)
                if s == 0:
                    ms[s][rr, 0:128] = dkv
                    ms[s][rr, 128:256] = jnp.where(low, dq, 0.0).astype(BF)
                else:
                    ms[s][rr, 0:128] = jnp.where(low, 0.0, dq).astype(BF)
                    ms[s][rr, 128:256] = dkv
            return 0

        lax.fori_loop(0, 2, body, 0)

        def back(t, carry):
            ga = mm(unsort_mat(2 * i, t), ms[0][...])
            gb = mm(unsort_mat(2 * i + 1, t), ms[1][...])
            out = jnp.concatenate(
                [ga[:, 0:128], ga[:, 128:256] + gb[:, 0:128], gb[:, 128:256]], axis=1
            )
            qkv[rows_of(t, 512), 384 * i : 384 * i + 384] = out.astype(BF)
            return carry + jnp.sum(out, axis=0, keepdims=True)

        return lax.fori_loop(0, 2, back, jnp.zeros((1, 384), F32))

    def gqkv(i):
        gw = mm(qkv[:, 384 * i : 384 * i + 384], xall[...], TN).astype(BF)
        for k, (u, rows) in enumerate(pair_rows(i)):
            g[0, u, rows, :] = gw[64 * k : 64 * k + 64, :]

    b0 = attend_back(0)
    gqkv(0)
    for u in range(2):
        g_step3(2, u)
    b1 = attend_back(1)
    gqkv(1)
    g_start(0, 0)
    for u in range(2):
        g_step2(1, u)
    b2 = attend_back(2)
    gqkv(2)
    g_start(0, 1)
    for u in range(2):
        g_step3(1, u)
    bs = (b0, b1, b2)
    rest = jnp.zeros((1, 384), F32)
    for u in range(2):
        heads = range(3 * u, 3 * u + 3)
        qs = [bs[h // 2][:, 128 + 64 * (h % 2) : 192 + 64 * (h % 2)] for h in heads]
        vs = [bs[h // 2][:, 64 + 192 * (h % 2) : 128 + 192 * (h % 2)] for h in heads]
        vb[0, pl.ds(10 + 2 * c + u, 1), :] = jnp.concatenate(qs + vs + [rest], axis=1)

    vdev = (
        (sib, z), (xn, z), (yn, z), (d, z + 1 - 2 * zj), (d, z + 2 - 4 * zc),
    )

    def v_send(k):
        rc(vb.at[k], vr.at[k], v_s.at[k], v_r.at[k], vdev[k]).start()

    def v_add(k):
        wait_recv(vr.at[k], v_r.at[k])
        vb[k + 1] = vb[k] + vr[k]

    v_send(0)
    partial(
        lambda rows, cols: mm(qkv[rows, :], wq[:, cols]),
        3,
    )

    def gin(m, _):
        rr = rows_of(m, 128)
        gtok[rr, :] = (fst[rr, :] + op[rr, :] + rcv[3, rr, :].astype(F32)).astype(BF)
        return 0

    lax.fori_loop(0, 4, gin, 0)
    v_add(0)
    v_send(1)
    g_step2(0, 0)
    v_add(1)
    v_send(2)
    g_step3(0, 0)
    v_add(2)
    v_send(3)
    g_step2(0, 1)
    v_add(3)
    v_send(4)
    g_step3(0, 1)
    tok_send(gtok, o2, 1)
    g_step4(2)
    g_step4(1)
    g_step5(2)
    g_step5(1)
    g_step6(2)
    g_step6(1)
    g_step4(0)
    g_step5(0)
    v_add(4)
    vout[...] = vb[5]
    vout[14:15, :] = vb[5, pl.ds(6 + z, 1), :]
    vout[15:16, :] = vb[5, pl.ds(10 + z, 1), :]
    g_step6(0)
    for a in range(3):
        g_end(a)
    tok_wait(tok, o1, 0)
    tok_wait(gtok, o2, 1)

    for a in range(1, 3):
        w_end(a)
    for k in range(4):
        wait_send(xrows(k, c), cx_s.at[k])
        if k >= 2:
            wait_send(rcv.at[k], pe_s.at[k])
    for k in (0, 2):
        wait_send(flow.at[pl.ds(0, 512)], pe_s.at[4 + k])
    for k in range(5):
        wait_send(vb.at[k], v_s.at[k])
    for j in range(2):

        @pl.when(jnp.logical_not(prim & (z == 2 * c + j)))
        def _(j=j):
            wait_send(ord_in, o_s.at[j])

    @pl.when(prim)
    def _():
        for k in range(3):
            wait_send(bias_in, b_s.at[k])
        wait_send(mr_in, m_s.at[0])
        wait_send(mg_in, m_s.at[1])


def layer(x, order, wqkv, wout, wb, wc, mr, mg, *small):
    dma = pltpu.SemaphoreType.DMA
    hbm = pl.BlockSpec(memory_space=pl.ANY)
    vmem = pl.BlockSpec(memory_space=pltpu.VMEM)
    V = pltpu.VMEM
    return pl.pallas_call(
        kernel,
        out_shape=(
            jax.ShapeDtypeStruct((2, 256, 768), BF),
            jax.ShapeDtypeStruct((2, 256, 768), BF),
            jax.ShapeDtypeStruct((768, 768), BF),
            jax.ShapeDtypeStruct((768, 768), BF),
            jax.ShapeDtypeStruct((768, 768), BF),
            jax.ShapeDtypeStruct((16, 768), F32),
        ),
        in_specs=[hbm] * 8 + [vmem] * 8,
        out_specs=(hbm, hbm, hbm, hbm, hbm, vmem),
        scratch_shapes=[
            V((1024, 768), BF),
            V((256, 2, 768), BF),
            V((2, 3, 2, 1024), jnp.int32),
            V((3, 2, 768, 768), BF),
            V((2, 8, 768), F32),
            V((8, 768), F32),
            V((8, 768), F32),
            V(mr.shape, jnp.int32),
            V(mg.shape, BF),
            V((mg.shape[0], 768), BF),
            V((1152, 768), BF),
            V((384, 768), BF),
            V((1024, 1152), BF),
            V((2, 1024, 128), jnp.int32),
            V((6, 1024, 128), BF),
            V((6, 1024, 128), BF),
            V((6, 1024, 128), F32),
            V((1024, 384), BF),
            V((2, 512, 768), BF),
            V((4, 512, 768), BF),
            V((512, 768), F32),
            V((512, 768), F32),
            V((512, 768), F32),
            V((512, 1), F32),
            V((1024, 768), BF),
            V((1024, 1536), BF),
            V((1024, 1536), BF),
            V((1024, 768), BF),
            V((3, 2, 768, 768), BF),
            V((3, 2, 2, 192, 768), BF),
            V((3, 2, 2, 96, 768), BF),
            V((3, 4, 96, 768), BF),
            V((3, 96, 768), BF),
            V((6, 16, 768), F32),
            V((5, 16, 768), F32),
            dma((2, 2)), dma((4,)), dma, dma((4,)), dma((4,)),
            dma((2,)), dma((2,)), dma,
            dma((3,)), dma((2,)), dma,
            dma((2,)), dma((2,)), dma((2,)),
            dma((3, 2, 2)), dma((3, 2, 2)), dma((2, 2)), dma((3, 2, 2)),
            dma((3, 2, 2, 3)), dma((3, 2, 2, 3)), dma((4,)),
            dma((7,)), dma((7,)), dma((4,)), dma((4,)),
            dma((2, 2)), dma((2, 2)), dma((2,)),
            dma((5,)), dma((5,)),
            dma((3, 2, 2)), dma((3, 2, 2)), dma((3, 2, 2)), dma((3, 2, 2)),
            dma((3, 2, 2)), dma((3, 4)), dma((3, 3)), dma((3, 3)), dma((3,)),
            dma((3, 4)), dma((3, 4)),
        ],
        compiler_params=pltpu.CompilerParams(
            collective_id=0, has_side_effects=True, vmem_limit_bytes=60 * 2**20
        ),
    )(x, order, wqkv, wout, wb, wc, mr, mg, *small)


def finish_kernel(
    o1, o2, ra, rb, rc, vec, out, gin, gq, go, gb, gc, fg, fs, ob, db, sg, ss, ub, qv,
    o1v, o2v, rv, outv, ginv, gv, in_sem, out_sem,
):
    loads = [
        pltpu.make_async_copy(a, b, in_sem.at[k])
        for k, (a, b) in enumerate(
            ((o1, o1v), (o2, o2v), (ra, rv.at[0]), (rb, rv.at[1]), (rc, rv.at[2]))
        )
    ]
    for k in (2, 3, 4, 1, 0):
        loads[k].start()
    stores = [
        pltpu.make_async_copy(a, b, out_sem.at[k])
        for k, (a, b) in enumerate(
            (
                (gv.at[0, pl.ds(0, 576)], gq), (gv.at[0, pl.ds(576, 192)], go),
                (gv.at[1], gb), (gv.at[2], gc), (ginv, gin), (outv, out),
            )
        )
    ]
    for ref, row in ((sg, 0), (ss, 1), (db, 2), (fg, 3), (fs, 4), (ob, 5), (ub, 14)):
        ref[...] = vec[row, :]
    wide = qv.shape[1]
    qv[0:1, :] = vec[15:16, 0:wide]
    qv[1:2, :] = vec[15:16, wide : 2 * wide]

    for a in range(3):
        loads[2 + a].wait()

        def body(k, _, a=a):
            rr = pl.ds(pl.multiple_of(k * 96, 96), 96)
            gv[a, rr, :] = rv[a, rr, :].astype(F32)
            return 0

        lax.fori_loop(0, 8, body, 0)
        if a == 0:
            stores[0].start()
            stores[1].start()
        else:
            stores[a + 1].start()

    def weave(src, dst, dtype):
        def body(k, _):
            rr = pl.ds(pl.multiple_of(k * 32, 32), 32)
            both = jnp.stack([src[0, rr, :].astype(F32), src[1, rr, :].astype(F32)], axis=1)
            dst[rr] = both.astype(dtype)
            return 0

        lax.fori_loop(0, 8, body, 0)

    loads[1].wait()
    weave(o2v, ginv, F32)
    stores[4].start()
    loads[0].wait()
    weave(o1v, outv, BF)
    stores[5].start()
    for cp in stores:
        cp.wait()


def finish(o1, o2, ra, rb, rc, vec):
    hbm = pl.BlockSpec(memory_space=pl.ANY)
    vmem = pl.BlockSpec(memory_space=pltpu.VMEM)
    V = pltpu.VMEM
    S = jax.ShapeDtypeStruct
    row = S((768,), F32)
    return pl.pallas_call(
        finish_kernel,
        out_shape=(
            S((256, 2, 768), BF), S((256, 2, 768), F32), S((576, 768), F32), S((192, 768), F32),
            S((768, 768), F32), S((768, 768), F32), row, row, row, row, row, row, row,
            S((2, 192), F32),
        ),
        in_specs=[hbm] * 5 + [vmem],
        out_specs=(hbm,) * 6 + (vmem,) * 8,
        scratch_shapes=[
            V((2, 256, 768), BF), V((2, 256, 768), BF), V((3, 768, 768), BF),
            V((256, 2, 768), BF), V((256, 2, 768), F32), V((3, 768, 768), F32),
            pltpu.SemaphoreType.DMA((5,)), pltpu.SemaphoreType.DMA((6,)),
        ],
        compiler_params=pltpu.CompilerParams(vmem_limit_bytes=60 * 2**20),
    )(o1, o2, ra, rb, rc, vec)


def shards(
    inputs, qkv_weight, qv_bias, out_weight, out_bias, first_gain, first_shift,
    first_layer_weight, first_layer_bias, second_layer_weight, second_layer_bias,
    second_gain, second_shift, cluster_order, masked_rows, masked_grad,
):
    t = lax.axis_index("tensor")
    heads = qkv_weight.shape[2]
    wqkv = qkv_weight.transpose(1, 2, 0).reshape(3 * heads, 768)
    order = cluster_order.transpose(1, 0, 2)

    o1, o2, ra, rb, rc, vec = layer(
        inputs, order, wqkv, out_weight, first_layer_weight, second_layer_weight,
        masked_rows, masked_grad.transpose(1, 0, 2), qv_bias,
        out_bias, first_gain, first_shift, second_layer_bias, second_gain, second_shift,
        first_layer_bias,
    )

    many = lax.axis_size("dp") // 8
    if many > 1:
        groups = [[8 * i + j for i in range(many)] for j in range(8)]
        ra, rb, rc = lax.psum(
            (ra.astype(F32), rb.astype(F32), rc.astype(F32)), "dp", axis_index_groups=groups
        )
        ra, rb, rc = ra.astype(BF), rb.astype(BF), rc.astype(BF)
        vec = lax.psum(vec, "dp", axis_index_groups=groups)
    outputs, grad_inputs, gq, go, gb, gc, fg, fs, ob, db, sg, ss, ub, qv = finish(
        o1, o2, ra, rb, rc, vec
    )
    return (
        outputs,
        grad_inputs,
        gq.reshape(3, heads, 768).transpose(2, 0, 1),
        qv,
        go,
        ob,
        fg,
        fs,
        gb,
        ub,
        gc,
        db,
        sg,
        ss,
    )


def solution(mesh):
    placed = (
        P("tensor", "dp", None), P(None, None, "tensor"), P(None, "tensor"), P("tensor", None),
        P(), P(), P(), P(None, "tensor"), P("tensor"), P("tensor", None), P(), P(), P(),
        P("dp", "tensor", None), P("dp", None), P("dp", None, None),
    )
    return jax.shard_map(
        shards,
        mesh=mesh,
        in_specs=placed,
        out_specs=(
            P("tensor", "dp", None), P("tensor", "dp", None), P(None, None, "tensor"),
            P(None, "tensor"), P("tensor", None), P(), P(), P(), P(None, "tensor"), P("tensor"),
            P("tensor", None), P(), P(), P(),
        ),
        check_vma=False,
    )
```
